256 devices in a mesh: ctx: 32 (over y_hi, z, core), dp: 8 (over y_lo, x).
Axes of the slice: x: 4, y: 4 (y_hi: 2, y_lo: 2; y = y_hi * 2 + y_lo), z: 8, core: 2. Of those that a mesh axis runs over, the one named last changes fastest.
Arguments:
- query_rows: bfloat16 [8, 8192, 512], P('dp', 'ctx'), may hold values from -25 to 25
- key_rows: bfloat16 [8, 8192, 512], P('dp', 'ctx'), may hold values from -25 to 25
- value_rows: bfloat16 [8, 8192, 512], P('dp', 'ctx'), may hold values from -20 to 20
- recordings: int32 [8, 32], P('dp'), may hold values from 0 to 3, never falling along the last dimension, each value on 1 to 11 neighbouring positions
- out_weight: bfloat16 [512, 1024], replicated, may hold values from -0.25 to 0.25
- cotangent: bfloat16 [8, 8192, 1024], P('dp', 'ctx'), may hold values from -12 to 12
Outputs:
- projected: bfloat16 [8, 8192, 1024], P('dp', 'ctx')
- grad_query: bfloat16 [8, 8192, 512], P('dp', 'ctx')
- grad_key: bfloat16 [8, 8192, 512], P('dp', 'ctx')
- grad_value: bfloat16 [8, 8192, 512], P('dp', 'ctx')
- grad_weight: bfloat16 [512, 1024], replicated
The draws below stay inside these ranges and needn't reach their ends.
Inputs may be any that keep to these rules, and one draw needn't show every extreme that they name: `recordings`: along the blocks of a batch the ids never fall; each recording covers 1 to 11 consecutive blocks, and some covers exactly 11.
All inputs are finite; a program needn't handle non-finite values.
Results may differ from the reference program's by a relative error of at most 0.02.
Values may be sent and summed in bfloat16 or wider, within the bound.
A program may use at most 128 MiB of HBM per device.

```python
import math
import jax
import jax.numpy as jnp
import numpy as np
from jax import lax

D = 1024
HEADS = 4
HEAD = 128
MOST = 11
TOK_DEV = 256
ATT = 512
BLOCKS = 32
BATCHES = 8
TOKENS = 8192
RECS = 4


def draw_query_rows(key, part):
    key = jax.random.fold_in(key, 11)
    return (1.2 * jnp.clip(jax.random.normal(key, (BATCHES, TOKENS, ATT)), -6.0, 6.0)).astype(jnp.bfloat16)


def draw_key_rows(key, part):
    key = jax.random.fold_in(key, 23)
    return (1.2 * jnp.clip(jax.random.normal(key, (BATCHES, TOKENS, ATT)), -6.0, 6.0)).astype(jnp.bfloat16)


def block_scale(rng, shape, pieces, least, largest):
    def one(axis_at, shards_of):
        draws = jax.random.uniform(jax.random.fold_in(jax.random.fold_in(rng, 6), axis_at), (shards_of,), jnp.float32, least / len(pieces), largest / len(pieces))
        return jnp.repeat(jnp.exp(draws), shape[axis_at] // shards_of).reshape((-1,) + (1,) * (len(shape) - axis_at - 1))

    gain = one(*pieces[0])
    for cut in pieces[1:]:
        gain = gain * one(*cut)
    return gain


def length_profile(amount, total, bound, skew):
    weights = [(1 << 20) // math.isqrt(rank ** skew) + 1 for rank in range(2, amount + 1)]
    surplus, holding = total - bound - (amount - 1), [1] * (amount - 1)
    while surplus > 0:
        free = [i for i in range(amount - 1) if holding[i] < bound]
        pool, budget = sum([weights[i] for i in free]), surplus
        for i in free:
            extra = min(bound - holding[i], max(1, budget * weights[i] // pool), surplus)
            holding[i] = holding[i] + extra
            surplus = surplus - extra
    return np.array([bound] + holding)


def ragged(key, number_of, total, reach, slope):
    if number_of == 2:
        one = jax.random.randint(key, (), max(1, total - reach), min(reach, total - 1) + 1)
        return jnp.stack([one, total - one])
    lengths = jnp.asarray(length_profile(number_of, total, reach, slope), jnp.int32)
    couples = (number_of - 1) // 2
    donor, receiver = lengths[1:1 + 2 * couples:2], lengths[2:2 + 2 * couples:2]
    margin = jnp.minimum(donor - 1, reach - receiver)
    moved = jax.random.randint(jax.random.fold_in(key, 1), (couples,), 0, 1 << 20) % (margin + 1)
    lengths = lengths.at[1:1 + 2 * couples:2].set(donor - moved).at[2:2 + 2 * couples:2].set(receiver + moved)
    return lengths[jax.random.permutation(jax.random.fold_in(key, 2), number_of)]


def gaussian(key, dims, spread, reach, shards=(), held_as=jnp.bfloat16):
    values = jax.random.normal(key, dims, jnp.float32) * spread
    if len(shards) > 0:
        values = block_scale(key, dims, shards, -0.22, 0.18) * values
    return jnp.clip(values, min=-reach, max=reach).astype(held_as)


def setup_inputs(seed: int = 0) -> dict:
    keys = jax.random.split(jax.random.key(seed), 7)
    query_rows = draw_query_rows(jax.random.fold_in(keys[6], 71), 0)
    key_rows = draw_key_rows(jax.random.fold_in(keys[6], 71), 0)
    value_rows = gaussian(keys[2], (BATCHES, TOKENS, ATT), 4.0, 20.0, ((0, 8), (1, 32)))
    recordings = jax.vmap(lambda own: jnp.searchsorted(jnp.cumsum(ragged(own, RECS, BLOCKS, MOST, 2)), jnp.arange(BLOCKS), side="right"))(jax.random.split(keys[3], BATCHES)).reshape((BATCHES, BLOCKS)).astype(jnp.int32)
    out_weight = gaussian(keys[4], (ATT, D), ATT ** -0.5, 0.25)
    cotangent = gaussian(keys[5], (BATCHES, TOKENS, D), 2.0, 12.0, ((0, 8), (1, 32)))
    return dict(query_rows=query_rows, key_rows=key_rows, value_rows=value_rows, recordings=recordings, out_weight=out_weight, cotangent=cotangent)


def heads_of(matrix):
    return matrix.reshape(-1, HEADS, HEAD).astype(jnp.float32)

def reference(query_rows, key_rows, value_rows, recordings, out_weight, cotangent):
    factor = 1.0 / math.sqrt(HEAD)
    reach_blocks = MOST - 1
    span_blocks = 2 * reach_blocks + 1
    item_ids = jnp.arange(BATCHES * BLOCKS, dtype=jnp.int32)

    def blocked(tensor):
        return tensor.reshape(BATCHES, BLOCKS, TOK_DEV, tensor.shape[-1])

    def padded(tensor):
        pad_widths = [(0, 0)] * tensor.ndim
        pad_widths[1] = (reach_blocks, reach_blocks)
        return jnp.pad(tensor, pad_widths)
    query_pad = padded(blocked(query_rows))
    key_pad = padded(blocked(key_rows))
    value_pad = padded(blocked(value_rows))
    label_pad = jnp.pad(recordings, ((0, 0), (reach_blocks, reach_blocks)), constant_values=-1)

    def window(source, batch_id, column_id):
        batch_row = lax.dynamic_index_in_dim(source, batch_id, 0, keepdims=False)
        return lax.dynamic_slice_in_dim(batch_row, column_id, span_blocks, 0)

    def centre(source, batch_id, column_id):
        batch_row = lax.dynamic_index_in_dim(source, batch_id, 0, keepdims=False)
        return lax.dynamic_index_in_dim(batch_row, column_id + reach_blocks, 0, keepdims=False)

    def valid_rows(batch_id, column_id):
        labels = window(label_pad, batch_id, column_id)
        own_label = centre(label_pad, batch_id, column_id)
        return jnp.repeat(labels == own_label, TOK_DEV)

    def forward_item(item_id):
        batch_id = item_id // BLOCKS
        column_id = item_id % BLOCKS
        valid_keys = valid_rows(batch_id, column_id)
        queries = heads_of(centre(query_pad, batch_id, column_id))
        key_window = heads_of(window(key_pad, batch_id, column_id).reshape(span_blocks * TOK_DEV, ATT))
        value_window = heads_of(window(value_pad, batch_id, column_id).reshape(span_blocks * TOK_DEV, ATT))
        scores = jnp.einsum('qhe,khe->hqk', queries, key_window) * factor
        scores = jnp.where(valid_keys[None, None, :], scores, -jnp.inf)
        row_max = lax.optimization_barrier(jnp.max(scores, axis=-1))
        raised = jnp.exp(scores - row_max[:, :, None])
        totals = lax.optimization_barrier(jnp.sum(raised, axis=-1))
        weights = lax.optimization_barrier(raised.astype(jnp.bfloat16)).astype(jnp.float32)
        summed = jnp.einsum('hqk,khe->qhe', weights, value_window) / totals.T[:, :, None]
        return (summed.reshape(TOK_DEV, ATT).astype(jnp.bfloat16), row_max + jnp.log(totals))
    attended, log_totals = lax.map(forward_item, item_ids)
    flat_att = attended.reshape(-1, ATT)
    flat_cot = cotangent.reshape(-1, D)
    log_totals = log_totals.reshape(BATCHES, BLOCKS, HEADS, TOK_DEV)
    projected = jnp.dot(flat_att, out_weight, preferred_element_type=jnp.float32).astype(jnp.bfloat16)
    projected = projected.reshape(BATCHES, TOKENS, D)
    grad_att = jnp.dot(flat_cot, out_weight.T, preferred_element_type=jnp.float32).astype(jnp.bfloat16)
    row_dots = lax.optimization_barrier(jnp.sum((grad_att.astype(jnp.float32) * flat_att.astype(jnp.float32)).reshape(BATCHES, BLOCKS, TOK_DEV, HEADS, HEAD), axis=-1))
    row_dots = row_dots.transpose(0, 1, 3, 2)
    grad_pad = padded(blocked(grad_att))
    total_pad = padded(log_totals)
    dots_pad = padded(row_dots)

    def query_item(item_id):
        batch_id = item_id // BLOCKS
        column_id = item_id % BLOCKS
        valid_keys = valid_rows(batch_id, column_id)
        queries = heads_of(centre(query_pad, batch_id, column_id))
        grad_heads = heads_of(centre(grad_pad, batch_id, column_id))
        log_total = centre(total_pad, batch_id, column_id)
        dot_rows = centre(dots_pad, batch_id, column_id)
        key_window = heads_of(window(key_pad, batch_id, column_id).reshape(span_blocks * TOK_DEV, ATT))
        value_window = heads_of(window(value_pad, batch_id, column_id).reshape(span_blocks * TOK_DEV, ATT))
        scores = jnp.einsum('qhe,khe->hqk', queries, key_window) * factor
        probable = jnp.where(valid_keys[None, None, :], jnp.exp(scores - log_total[:, :, None]), 0.0)
        grad_probs = jnp.einsum('qhe,khe->hqk', grad_heads, value_window)
        grad_scores = lax.optimization_barrier((probable * (grad_probs - dot_rows[:, :, None])).astype(jnp.bfloat16)).astype(jnp.float32)
        result = jnp.einsum('hqk,khe->qhe', grad_scores, key_window) * factor
        return result.reshape(TOK_DEV, ATT).astype(jnp.bfloat16)

    def key_item(item_id):
        batch_id = item_id // BLOCKS
        column_id = item_id % BLOCKS
        valid_queries = valid_rows(batch_id, column_id)
        keys_own = heads_of(centre(key_pad, batch_id, column_id))
        values_own = heads_of(centre(value_pad, batch_id, column_id))
        query_window = heads_of(window(query_pad, batch_id, column_id).reshape(span_blocks * TOK_DEV, ATT))
        grad_window = heads_of(window(grad_pad, batch_id, column_id).reshape(span_blocks * TOK_DEV, ATT))
        total_window = window(total_pad, batch_id, column_id).transpose(1, 0, 2).reshape(HEADS, span_blocks * TOK_DEV)
        dots_window = window(dots_pad, batch_id, column_id).transpose(1, 0, 2).reshape(HEADS, span_blocks * TOK_DEV)
        scores = jnp.einsum('qhe,khe->hqk', query_window, keys_own) * factor
        probable = jnp.where(valid_queries[None, :, None], jnp.exp(scores - total_window[:, :, None]), 0.0)
        rounded = lax.optimization_barrier(probable.astype(jnp.bfloat16)).astype(jnp.float32)
        grad_values = jnp.einsum('hqk,qhe->khe', rounded, grad_window)
        grad_probs = jnp.einsum('qhe,khe->hqk', grad_window, values_own)
        grad_scores = lax.optimization_barrier((probable * (grad_probs - dots_window[:, :, None])).astype(jnp.bfloat16)).astype(jnp.float32)
        grad_keys = jnp.einsum('hqk,qhe->khe', grad_scores, query_window) * factor
        return (grad_keys.reshape(TOK_DEV, ATT).astype(jnp.bfloat16), grad_values.reshape(TOK_DEV, ATT).astype(jnp.bfloat16))
    grad_query = lax.map(query_item, item_ids).reshape(BATCHES, TOKENS, ATT)
    grad_key, grad_value = lax.map(key_item, item_ids)
    grad_key = grad_key.reshape(BATCHES, TOKENS, ATT)
    grad_value = grad_value.reshape(BATCHES, TOKENS, ATT)
    weight_part = lax.dot_general(flat_att, flat_cot, (((0,), (0,)), ((), ())), preferred_element_type=jnp.float32)
    grad_weight = (weight_part / math.sqrt(BATCHES * TOKENS)).astype(jnp.bfloat16)
    return (projected, grad_query, grad_key, grad_value, grad_weight)
```

```python
import functools
import math

import jax
import jax.numpy as jnp
from jax import lax
from jax.experimental import pallas as pl
from jax.experimental.pallas import tpu as pltpu
from jax.sharding import PartitionSpec as P

HEADS = 4
HEAD = 128
MOST = 11
TOK = 256
D = 1024
ATT = 512
WINDOW = 26
CROSS = 5
FACTOR = 1.0 / math.sqrt(HEAD)
SCALE2 = FACTOR * math.log2(math.e)
FAR = 1e30
MESH = pl.DeviceIdType.MESH
F32 = jnp.float32
BF16 = jnp.bfloat16


def dot(a, b, dims):
    return lax.dot_general(a, b, (dims, ((), ())), preferred_element_type=F32)


NT = ((1,), (1,))
NN = ((1,), (0,))
TN = ((0,), (0,))


def kernel(
    start_ref, count_ref, q_ref, k_ref, v_ref, cot_ref, w_ref,
    proj_ref, gq_ref, gk_ref, gv_ref, gw_ref,
    kv, qd, pack_kv, pack_q, pack_d, stats, lse_col, dot_col, scores,
    out_send, out_home, grad_send, grad_home,
    wp, wc, rc, wx, rx, wy, ry, rz, fz, gwf,
    s1_s, s1_r, s2_s, s2_r, c1_s, c1_r, c2_s, c2_r, s3_s, s3_r, cx_s, cx_r,
    st_s, st_r, o_s, o_r, g_s, g_r, ar_s, ar_r, az_s, az_r,
):
    ctx = lax.axis_index("ctx")
    dp = lax.axis_index("dp")
    yh, z, core = ctx // 16, (ctx // 2) % 8, ctx % 2
    yl, x = dp // 4, dp % 4
    y = yh * 2 + yl
    side = 2 * (z % 2) - 1
    head = z // 2
    partner = (z - side + 8) % 8

    def at(yh_=None, z_=None, core_=None):
        a = yh if yh_ is None else yh_
        b = z if z_ is None else z_
        c = core if core_ is None else core_
        return (a * 16 + b * 2 + c, dp)

    def at_x(o):
        return (ctx, yl * 4 + (x + o) % 4)

    def at_y(o):
        y2 = (y + o) % 4
        return ((y2 // 2) * 16 + z * 2 + core, (y2 % 2) * 4 + x)

    other_core = at(core_=1 - core)
    other_row = at(yh_=1 - yh)
    near = at(z_=partner)

    def own_z(k):
        return (z + side * k + 8) % 8

    def their_z(k):
        return (z - side * (k + 1) + 8) % 8

    def slot(zz, cc):
        return 10 * yh + 2 * zz + cc

    targets = [None, (z + side + 8) % 8, (z - 2 * side + 8) % 8, (z + 3 * side + 8) % 8]

    def remote(src, dst, ss, rs, device):
        return pltpu.make_async_remote_copy(
            src_ref=src, dst_ref=dst, send_sem=ss, recv_sem=rs, device_id=device, device_id_type=MESH
        )

    peers = [other_core, at(z_=partner, core_=1 - core)]
    peers += [at(z_=(z + o) % 8) for o in range(1, 8)]
    peers += [at_x(o) for o in range(1, 4)]
    peers += [at_y(o) for o in range(1, 4)]
    peers += [
        at(1 - yh, z, 1 - core),
        at(1 - yh, partner, core),
        at(1 - yh, partner, 1 - core),
    ]
    barrier = pltpu.get_barrier_semaphore()
    for peer in peers:
        pl.semaphore_signal(barrier, inc=1, device_id=peer, device_id_type=MESH)
    for h in range(HEADS):
        cols = slice(h * HEAD, (h + 1) * HEAD)
        pack_kv[h, 0] = k_ref[:, cols]
        pack_kv[h, 1] = v_ref[:, cols]
        pack_q[h] = q_ref[:, cols]
    pl.semaphore_wait(barrier, len(peers))

    home = slot(z, core)

    def leg1(kind, k):
        t = targets[k]
        if kind == 0:
            src, dst = pack_kv.at[t // 2], kv.at[home]
        elif kind == 1:
            src, dst = pack_q.at[t // 2], qd.at[home, 0]
        else:
            src, dst = pack_d.at[t // 2], qd.at[home, 1]
        return remote(src, dst, s1_s.at[kind, k], s1_r.at[kind, k], at(z_=t))

    for kind in (0, 1):
        for k in (1, 2, 3):
            leg1(kind, k).start()
    kv[home] = pack_kv[head]
    qd[home, 0] = pack_q[head]

    bufs = (kv, qd)

    def leg2(g, k):
        sl = slot(own_z(k), core)
        return remote(bufs[g].at[sl], bufs[g].at[sl], s2_s.at[g, k], s2_r.at[g, k], near)

    def core1(g, k):
        sl = slot(own_z(k), core)
        return remote(bufs[g].at[sl], bufs[g].at[sl], c1_s.at[g, k], c1_r.at[g, k], other_core)

    def core2(g, k):
        sl = slot(their_z(k), core)
        return remote(bufs[g].at[sl], bufs[g].at[sl], c2_s.at[g, k], c2_r.at[g, k], other_core)

    def leg3(g, m):
        src = slot(m + 3 * (1 - yh), core)
        dst = 2 * m + core + 16 * yh
        return remote(bufs[g].at[src], bufs[g].at[dst], s3_s.at[g, m], s3_r.at[g, m], other_row)

    def cross_core(g, m):
        sl = 2 * m + core + 16 * (1 - yh)
        return remote(bufs[g].at[sl], bufs[g].at[sl], cx_s.at[g, m], cx_r.at[g, m], other_core)

    def maybe_leg3(g, zz):
        m = zz - 3 * (1 - yh)

        @pl.when(jnp.logical_and(m >= 0, m < CROSS))
        def _():
            leg3(g, m).start()

    def spread_own(g, k):
        leg2(g, k).start()
        maybe_leg3(g, own_z(k))
        core1(g, k).start()

    def spread_their(g, k):
        leg2(g, k).wait_recv()
        maybe_leg3(g, their_z(k))
        core2(g, k).start()

    def spread_cross(g, m):
        leg3(g, m).wait_recv()
        cross_core(g, m).start()

    def all_here(g):
        for k in range(4):
            core1(g, k).wait_recv()
            core2(g, k).wait_recv()
        for m in range(CROSS):
            cross_core(g, m).wait_recv()

    spread_own(0, 0)
    grad_att = dot(cot_ref[...], w_ref[...], NT).astype(BF16)
    for h in range(HEADS):
        pack_d[h] = grad_att[:, h * HEAD : (h + 1) * HEAD]
    qd[home, 1] = pack_d[head]
    for k in (1, 2, 3):
        leg1(0, k).wait_recv()
        spread_own(0, k)
    for k in (1, 2, 3):
        leg1(2, k).start()
    for k in range(4):
        spread_their(0, k)
    for m in range(CROSS):
        spread_cross(0, m)
    for k in (1, 2, 3):
        leg1(1, k).wait_recv()
        leg1(2, k).wait_recv()
    all_here(0)

    member = yh * 4 + (z % 2) * 2 + core

    def send_out(k):
        return remote(out_send.at[k], out_home.at[head], o_s.at[k], o_r.at[k], at(z_=own_z(k)))

    def block_range(k):
        block = 16 * yh + 2 * own_z(k) + core
        return start_ref[block] - 6 * yh, count_ref[block]

    def nth(first, count, t):
        return jnp.clip(first + jnp.minimum(t, count - 1), 0, WINDOW - 1)

    def pen(t, count):
        return jnp.where(t < count, 0.0, FAR)

    def forward_block(k, carry):
        @pl.when(k == 0)
        def _():
            for j in range(4):
                spread_own(1, j)

        sl = slot(own_z(k), core)
        first, count = block_range(k)
        query = qd[sl, 0]
        top = None
        for t in range(MOST):
            other = nth(first, count, t)
            s = dot(query, kv[other, 0], NT)
            scores[t] = s
            top = s if top is None else jnp.maximum(top, s)
        peak = jnp.max(top, axis=1, keepdims=True) * SCALE2
        total = jnp.zeros((TOK, HEAD), F32)
        acc = jnp.zeros((TOK, HEAD), F32)
        for t in range(MOST):
            other = nth(first, count, t)
            p = jnp.exp2(scores[t] * SCALE2 - (peak + pen(t, count)))
            total = total + (p[:, :HEAD] + p[:, HEAD:])
            acc = acc + dot(p.astype(BF16), kv[other, 1], NN)
        sums = jnp.sum(total, axis=1, keepdims=True)
        attended = (acc / sums).astype(BF16)
        out_send[k] = attended
        lse = peak + jnp.log2(sums)
        rd = jnp.sum(qd[sl, 1].astype(F32) * attended.astype(F32), axis=1, keepdims=True)
        lse_col[k] = jnp.broadcast_to(lse, (TOK, HEAD))
        dot_col[k] = jnp.broadcast_to(rd, (TOK, HEAD))
        lane = lax.broadcasted_iota(jnp.int32, (TOK, HEAD), 1)
        turned = jnp.where(lane < 8, lse, rd).T
        stats[member, k] = turned[:16]

        @pl.when(k == 0)
        def _():
            out_home[head] = out_send[0]

        @pl.when(k > 0)
        def _():
            send_out(k).start()

        @pl.when(k == 1)
        def _():
            for j in range(4):
                spread_their(1, j)

        @pl.when(k == 3)
        def _():
            for m in range(CROSS):
                spread_cross(1, m)

        return carry

    lax.fori_loop(0, 4, forward_block, 0)

    quad = [
        other_core, near, at(z_=partner, core_=1 - core), other_row,
        at(1 - yh, z, 1 - core), at(1 - yh, partner, core), at(1 - yh, partner, 1 - core),
    ]

    def send_stats(i):
        return remote(stats.at[member], stats.at[member], st_s.at[i], st_r.at[i], quad[i])

    for i in range(7):
        send_stats(i).start()

    def home_out(k):
        t = targets[k]
        return remote(out_send.at[k], out_home.at[t // 2], o_s.at[k], o_r.at[k], at(z_=t))

    def ar_core():
        return remote(wp.at[1 - core], rc, ar_s.at[0], ar_r.at[0], other_core)

    def ar_x(o):
        return remote(wc.at[(x + o) % 4], rx.at[o - 1], ar_s.at[o], ar_r.at[o], at_x(o))

    def ar_y(o):
        return remote(wx.at[(y + o) % 4], ry.at[o - 1], ar_s.at[3 + o], ar_r.at[3 + o], at_y(o))

    def ar_z(o):
        t = (z + o) % 8
        return remote(wy.at[t], rz.at[o - 1], az_s.at[0, o], az_r.at[0, o], at(z_=t))

    def back_z(o):
        return remote(fz.at[z], fz.at[z], az_s.at[1, o], az_r.at[1, o], at(z_=(z + o) % 8))

    def back_y(o):
        part = gwf.at[core, x, y]
        return remote(part, part, ar_s.at[6 + o], ar_r.at[6 + o], at_y(o))

    def back_x(o):
        part = gwf.at[core, x]
        return remote(part, part, ar_s.at[9 + o], ar_r.at[9 + o], at_x(o))

    def back_core():
        return remote(gwf.at[core], gwf.at[core], ar_s.at[13], ar_r.at[13], other_core)

    def weight_term():
        for k in (1, 2, 3):
            home_out(k).wait_recv()
        for h in range(HEADS):
            part = dot(out_home[h], cot_ref[...], TN).astype(BF16)
            for piece in range(8):
                row = h * 8 + piece
                wp[row // 16, (row // 4) % 4, row % 4] = part[piece * 16 : (piece + 1) * 16]
        ar_core().start()

    def sum_core():
        ar_core().wait_recv()
        wc[...] = (wp[core].astype(F32) + rc[...].astype(F32)).astype(BF16)
        for o in (1, 2, 3):
            ar_x(o).start()

    def sum_x():
        total = wc[x].astype(F32)
        for o in (1, 2, 3):
            ar_x(o).wait_recv()
            total = total + rx[o - 1].astype(F32)
        wx[...] = total.astype(BF16)
        for o in (1, 2, 3):
            ar_y(o).start()

    def sum_y():
        total = wx[y].astype(F32)
        for o in (1, 2, 3):
            ar_y(o).wait_recv()
            total = total + ry[o - 1].astype(F32)
        total = total.astype(BF16)
        for j in range(8):
            wy[j] = total[:, j * HEAD : (j + 1) * HEAD]
        for o in range(1, 8):
            ar_z(o).start()

    def sum_z():
        total = wy[z].astype(F32)
        for o in range(1, 8):
            ar_z(o).wait_recv()
            total = total + rz[o - 1].astype(F32)
        rows = TOK * lax.axis_size("ctx") * lax.axis_size("dp")
        fz[z] = (total * (1.0 / math.sqrt(rows))).astype(BF16)
        for o in range(1, 8):
            back_z(o).start()

    def gather_z():
        for o in range(1, 8):
            back_z(o).wait_recv()
        for j in range(8):
            gwf[core, x, y, :, j * HEAD : (j + 1) * HEAD] = fz[j]
        for o in (1, 2, 3):
            back_y(o).start()

    def gather_y():
        for o in (1, 2, 3):
            back_y(o).wait_recv()
        for o in (1, 2, 3):
            back_x(o).start()

    def gather_x():
        for o in (1, 2, 3):
            back_x(o).wait_recv()
        back_core().start()

    def send_grad(a, k):
        return remote(
            grad_send.at[a, k], grad_home.at[a, head], g_s.at[a, k], g_r.at[a, k], at(z_=own_z(k))
        )

    def give_grad(a, k, value):
        grad_send[a, k] = value

        @pl.when(k == 0)
        def _():
            grad_home[a, head] = grad_send[a, 0]

        @pl.when(k > 0)
        def _():
            send_grad(a, k).start()

    def query_block(k, carry):
        @pl.when(k == 2)
        def _():
            weight_term()

        @pl.when(k == 3)
        def _():
            sum_core()

        sl = slot(own_z(k), core)
        first, count = block_range(k)
        query, grad = qd[sl, 0], qd[sl, 1]
        lse = lse_col[k][:, :1]
        rd = dot_col[k][:, :1]
        acc = jnp.zeros((TOK, HEAD), F32)
        for t in range(MOST):
            other = nth(first, count, t)
            keys = kv[other, 0]
            p = jnp.exp2(dot(query, keys, NT) * SCALE2 - (lse + pen(t, count)))
            ds = (p * (dot(grad, kv[other, 1], NT) - rd)).astype(BF16)
            acc = acc + dot(ds, keys, NN)
        give_grad(0, k, (acc * FACTOR).astype(BF16))
        return carry

    lax.fori_loop(0, 4, query_block, 0)

    all_here(1)
    for i in range(7):
        send_stats(i).wait_recv()

    def key_block(k, carry):
        @pl.when(k == 0)
        def _():
            sum_x()

        @pl.when(k == 1)
        def _():
            sum_y()

        @pl.when(k == 2)
        def _():
            sum_z()

        @pl.when(k == 3)
        def _():
            gather_z()

        sl = slot(own_z(k), core)
        first, count = block_range(k)
        keys, values = kv[sl, 0], kv[sl, 1]
        acc_k = jnp.zeros((TOK, HEAD), F32)
        acc_v = jnp.zeros((TOK, HEAD), F32)
        for t in range(MOST):
            other = nth(first, count, t)
            block = other + 6 * yh
            oz = (block // 2) % 8
            left = (2 * head - oz + 8) % 8
            in_left = left < 4
            k_of = jnp.where(in_left, left, 7 - left)
            who = (block // 16) * 4 + jnp.where(in_left, 0, 2) + block % 2
            lse = stats[who, k_of, 0:1, :]
            rd = stats[who, k_of, 8:9, :]
            query, grad = qd[other, 0], qd[other, 1]
            p = jnp.exp2(dot(keys, query, NT) * SCALE2 - (lse + pen(t, count)))
            acc_v = acc_v + dot(p.astype(BF16), grad, NN)
            ds = (p * (dot(values, grad, NT) - rd)).astype(BF16)
            acc_k = acc_k + dot(ds, query, NN)
        give_grad(1, k, (acc_k * FACTOR).astype(BF16))
        give_grad(2, k, acc_v.astype(BF16))
        return carry

    lax.fori_loop(0, 4, key_block, 0)

    gather_y()
    projected = dot(out_home[0], w_ref[0:HEAD], NN)
    for h in range(1, HEADS):
        projected = projected + dot(out_home[h], w_ref[h * HEAD : (h + 1) * HEAD], NN)
    proj_ref[...] = projected.astype(BF16)
    gather_x()

    def home_grad(a, k):
        t = targets[k]
        return remote(
            grad_send.at[a, k], grad_home.at[a, t // 2], g_s.at[a, k], g_r.at[a, k], at(z_=t)
        )

    for a, ref in enumerate((gq_ref, gk_ref, gv_ref)):
        for k in (1, 2, 3):
            home_grad(a, k).wait_recv()
        for h in range(HEADS):
            ref[:, h * HEAD : (h + 1) * HEAD] = grad_home[a, h]
    back_core().wait_recv()
    for a in range(2):
        for b in range(4):
            for c in range(4):
                row = a * 256 + b * 64 + c * 16
                gw_ref[row : row + 16] = gwf[a, b, c]

    for k in (1, 2, 3):
        for kind in range(3):
            leg1(kind, k).wait_send()
        send_out(k).wait_send()
        for a in range(3):
            send_grad(a, k).wait_send()
    for g in range(2):
        for k in range(4):
            leg2(g, k).wait_send()
            core1(g, k).wait_send()
            core2(g, k).wait_send()
        for m in range(CROSS):
            leg3(g, m).wait_send()
            cross_core(g, m).wait_send()
    for i in range(7):
        send_stats(i).wait_send()
    ar_core().wait_send()
    for o in (1, 2, 3):
        for make in (ar_x, ar_y, back_y, back_x):
            make(o).wait_send()
    for o in range(1, 8):
        ar_z(o).wait_send()
        back_z(o).wait_send()
    back_core().wait_send()


def on_device(query_rows, key_rows, value_rows, recordings, out_weight, cotangent):
    labels = recordings[0]
    start = jnp.sum(labels[None, :] < labels[:, None], axis=1).astype(jnp.int32)
    count = jnp.sum(labels[None, :] == labels[:, None], axis=1).astype(jnp.int32)
    vmem = pl.BlockSpec(memory_space=pltpu.VMEM)
    smem = pl.BlockSpec(memory_space=pltpu.SMEM)
    dma = pltpu.SemaphoreType.DMA
    outs = pl.pallas_call(
        kernel,
        out_shape=(
            jax.ShapeDtypeStruct((TOK, D), BF16),
            jax.ShapeDtypeStruct((TOK, ATT), BF16),
            jax.ShapeDtypeStruct((TOK, ATT), BF16),
            jax.ShapeDtypeStruct((TOK, ATT), BF16),
            jax.ShapeDtypeStruct((ATT, D), BF16),
        ),
        in_specs=[smem, smem, vmem, vmem, vmem, vmem, vmem],
        out_specs=(vmem,) * 5,
        scratch_shapes=[
            pltpu.VMEM((WINDOW, 2, TOK, HEAD), BF16),
            pltpu.VMEM((WINDOW, 2, TOK, HEAD), BF16),
            pltpu.VMEM((HEADS, 2, TOK, HEAD), BF16),
            pltpu.VMEM((HEADS, TOK, HEAD), BF16),
            pltpu.VMEM((HEADS, TOK, HEAD), BF16),
            pltpu.VMEM((8, 4, 16, TOK), F32),
            pltpu.VMEM((4, TOK, HEAD), F32),
            pltpu.VMEM((4, TOK, HEAD), F32),
            pltpu.VMEM((MOST, TOK, TOK), F32),
            pltpu.VMEM((4, TOK, HEAD), BF16),
            pltpu.VMEM((HEADS, TOK, HEAD), BF16),
            pltpu.VMEM((3, 4, TOK, HEAD), BF16),
            pltpu.VMEM((3, HEADS, TOK, HEAD), BF16),
            pltpu.VMEM((2, 4, 4, 16, D), BF16),
            pltpu.VMEM((4, 4, 16, D), BF16),
            pltpu.VMEM((4, 4, 16, D), BF16),
            pltpu.VMEM((4, 16, D), BF16),
            pltpu.VMEM((3, 4, 16, D), BF16),
            pltpu.VMEM((8, 16, HEAD), BF16),
            pltpu.VMEM((3, 16, D), BF16),
            pltpu.VMEM((7, 16, HEAD), BF16),
            pltpu.VMEM((8, 16, HEAD), BF16),
            pltpu.VMEM((2, 4, 4, 16, D), BF16),
        ]
        + [dma((3, 4))] * 2
        + [dma((2, 4))] * 6
        + [dma((2, CROSS))] * 4
        + [dma((7,))] * 2
        + [dma((4,))] * 2
        + [dma((3, 4))] * 2
        + [dma((14,))] * 2
        + [dma((2, 8))] * 2,
        compiler_params=pltpu.CompilerParams(
            collective_id=0, has_side_effects=True, vmem_limit_bytes=56 << 20
        ),
    )(start, count, query_rows[0], key_rows[0], value_rows[0], cotangent[0], out_weight)
    projected, grad_query, grad_key, grad_value, grad_weight = outs
    return (projected[None], grad_query[None], grad_key[None], grad_value[None], grad_weight)


def solution(mesh):
    rows = P("dp", "ctx", None)
    return jax.shard_map(
        on_device,
        mesh=mesh,
        in_specs=(rows, rows, rows, P("dp", None), P(), rows),
        out_specs=(rows, rows, rows, rows, P()),
        check_vma=False,
    )
```

```python
import functools
import math

import jax
import jax.numpy as jnp
from jax import lax
from jax.experimental import pallas as pl
from jax.experimental.pallas import tpu as pltpu
from jax.sharding import PartitionSpec as P

HEADS = 4
HEAD = 128
MOST = 11
TOK = 256
D = 1024
ATT = 512
BLOCKS = 32
WINDOW = 26
CROSS = 5
FACTOR = 1.0 / math.sqrt(HEAD)
SCALE2 = FACTOR * math.log2(math.e)
FAR = 1e30
MESH = pl.DeviceIdType.MESH
F32 = jnp.float32
BF16 = jnp.bfloat16


def dot(a, b, dims):
    return lax.dot_general(a, b, (dims, ((), ())), preferred_element_type=F32)


NT = ((1,), (1,))
NN = ((1,), (0,))
TN = ((0,), (0,))


def kernel(
    rec_ref, q_hbm, k_hbm, v_hbm, cot_hbm, w_hbm,
    proj_hbm, gq_hbm, gk_hbm, gv_hbm, gw_hbm,
    cot_ref, w_ref, proj_ref, ranges,
    kv, qd, pack_kv, pack_q, pack_d, stats, lse_col, dot_col, scores,
    out_send, out_home, grad_send, grad_home,
    wp, wc, rc, wx, rx, rxy, wz, rz, fz, gwf,
    s1_s, s1_r, s2_s, s2_r, c1_s, c1_r, c2_s, c2_r, s3_s, s3_r, cx_s, cx_r,
    st_s, st_r, o_s, o_r, g_s, g_r, ar_s, ar_r, az_s, az_r, wb_s, wb_r, in_s, out_s,
):
    ctx = lax.axis_index("ctx")
    dp = lax.axis_index("dp")
    yh, z, core = ctx // 16, (ctx // 2) % 8, ctx % 2
    yl, x = dp // 4, dp % 4
    y = yh * 2 + yl
    side = 2 * (z % 2) - 1
    head = z // 2
    partner = (z - side + 8) % 8

    def at(yh_=None, z_=None, core_=None):
        a = yh if yh_ is None else yh_
        b = z if z_ is None else z_
        c = core if core_ is None else core_
        return (a * 16 + b * 2 + c, dp)

    def at_x(o):
        return (ctx, yl * 4 + (x + o) % 4)

    def at_y(o):
        y2 = (y + o) % 4
        return ((y2 // 2) * 16 + z * 2 + core, (y2 % 2) * 4 + x)

    other_core = at(core_=1 - core)
    other_row = at(yh_=1 - yh)
    near = at(z_=partner)

    def own_z(k):
        return (z + side * k + 8) % 8

    def their_z(k):
        return (z - side * (k + 1) + 8) % 8

    def slot(zz, cc):
        return 10 * yh + 2 * zz + cc

    targets = [None, (z + side + 8) % 8, (z - 2 * side + 8) % 8, (z + 3 * side + 8) % 8]

    def remote(src, dst, ss, rs, device):
        return pltpu.make_async_remote_copy(
            src_ref=src, dst_ref=dst, send_sem=ss, recv_sem=rs, device_id=device, device_id_type=MESH
        )

    loads = []
    for h in range(HEADS):
        cols = pl.ds(h * HEAD, HEAD)
        loads.append((k_hbm.at[:, cols], pack_kv.at[h, 0]))
        loads.append((v_hbm.at[:, cols], pack_kv.at[h, 1]))
        loads.append((q_hbm.at[:, cols], pack_q.at[h]))
    loads += [(cot_hbm, cot_ref), (w_hbm, w_ref)]
    loads = [pltpu.make_async_copy(src, dst, in_s.at[i]) for i, (src, dst) in enumerate(loads)]
    for load in loads:
        load.start()

    peers = [other_core, at(z_=partner, core_=1 - core)]
    peers += [at(z_=(z + o) % 8) for o in range(1, 8)]
    peers += [at_x(o) for o in range(1, 4)]
    peers += [at_y(o) for o in range(1, 4)]
    peers += [
        at(1 - yh, z, 1 - core),
        at(1 - yh, partner, core),
        at(1 - yh, partner, 1 - core),
    ]
    barrier = pltpu.get_barrier_semaphore()
    for peer in peers:
        pl.semaphore_signal(barrier, inc=1, device_id=peer, device_id_type=MESH)
    for k in range(4):
        label = rec_ref[0, 16 * yh + 2 * own_z(k) + core]
        first = jnp.int32(0)
        count = jnp.int32(0)
        for j in range(BLOCKS):
            first = first + jnp.where(rec_ref[0, j] < label, 1, 0)
            count = count + jnp.where(rec_ref[0, j] == label, 1, 0)
        ranges[0, k] = first - 6 * yh
        ranges[1, k] = count
    for load in loads[:12]:
        load.wait()
    pl.semaphore_wait(barrier, len(peers))

    home = slot(z, core)

    def leg1(kind, k):
        t = targets[k]
        if kind == 0:
            src, dst = pack_kv.at[t // 2], kv.at[home]
        elif kind == 1:
            src, dst = pack_q.at[t // 2], qd.at[home, 0]
        else:
            src, dst = pack_d.at[t // 2], qd.at[home, 1]
        return remote(src, dst, s1_s.at[kind, k], s1_r.at[kind, k], at(z_=t))

    for kind in (0, 1):
        for k in (1, 2, 3):
            leg1(kind, k).start()
    kv[home] = pack_kv[head]
    qd[home, 0] = pack_q[head]

    bufs = (kv, qd)

    def leg2(g, k):
        sl = slot(own_z(k), core)
        return remote(bufs[g].at[sl], bufs[g].at[sl], s2_s.at[g, k], s2_r.at[g, k], near)

    def core1(g, k):
        sl = slot(own_z(k), core)
        return remote(bufs[g].at[sl], bufs[g].at[sl], c1_s.at[g, k], c1_r.at[g, k], other_core)

    def core2(g, k):
        sl = slot(their_z(k), core)
        return remote(bufs[g].at[sl], bufs[g].at[sl], c2_s.at[g, k], c2_r.at[g, k], other_core)

    def leg3(g, m):
        src = slot(m + 3 * (1 - yh), core)
        dst = 2 * m + core + 16 * yh
        return remote(bufs[g].at[src], bufs[g].at[dst], s3_s.at[g, m], s3_r.at[g, m], other_row)

    def cross_core(g, m):
        sl = 2 * m + core + 16 * (1 - yh)
        return remote(bufs[g].at[sl], bufs[g].at[sl], cx_s.at[g, m], cx_r.at[g, m], other_core)

    def maybe_leg3(g, zz):
        m = zz - 3 * (1 - yh)

        @pl.when(jnp.logical_and(m >= 0, m < CROSS))
        def _():
            leg3(g, m).start()

    def spread_row(g, k):
        leg2(g, k).start()
        core1(g, k).start()

    def spread_own(g, k):
        spread_row(g, k)
        maybe_leg3(g, own_z(k))

    def spread_their(g, k):
        leg2(g, k).wait_recv()
        maybe_leg3(g, their_z(k))
        core2(g, k).start()

    def spread_cross(g, m):
        leg3(g, m).wait_recv()
        cross_core(g, m).start()

    def all_here(g):
        for k in range(4):
            core1(g, k).wait_recv()
            core2(g, k).wait_recv()
        for m in range(CROSS):
            cross_core(g, m).wait_recv()

    spread_own(0, 0)
    for load in loads[12:]:
        load.wait()
    grad_att = dot(cot_ref[...], w_ref[...], NT).astype(BF16)
    for h in range(HEADS):
        pack_d[h] = grad_att[:, h * HEAD : (h + 1) * HEAD]
    qd[home, 1] = pack_d[head]
    for k in (1, 2, 3):
        leg1(2, k).start()
    for k in (1, 2, 3):
        leg1(0, k).wait_recv()
        spread_own(0, k)
    for k in range(4):
        spread_their(0, k)
    spread_row(1, 0)
    for k in (1, 2, 3):
        leg1(1, k).wait_recv()
        leg1(2, k).wait_recv()
        spread_row(1, k)
    for m in range(CROSS):
        spread_cross(0, m)
    for k in range(4):
        maybe_leg3(1, own_z(k))
    all_here(0)

    member = yh * 4 + (z % 2) * 2 + core

    def send_out(k):
        return remote(out_send.at[k], out_home.at[head], o_s.at[k], o_r.at[k], at(z_=own_z(k)))

    def block_range(k):
        return ranges[0, k], ranges[1, k]

    def nth(first, count, t):
        return jnp.clip(first + jnp.minimum(t, count - 1), 0, WINDOW - 1)

    def pen(t, count):
        return jnp.where(t < count, 0.0, FAR)

    def forward_block(k, carry):
        sl = slot(own_z(k), core)
        first, count = block_range(k)
        query = qd[sl, 0]
        top = None
        for t in range(MOST):
            other = nth(first, count, t)
            s = dot(query, kv[other, 0], NT)
            scores[t] = s
            top = s if top is None else jnp.maximum(top, s)
        peak = jnp.max(top, axis=1, keepdims=True) * SCALE2
        total = jnp.zeros((TOK, HEAD), F32)
        acc = jnp.zeros((TOK, HEAD), F32)
        for t in range(MOST):
            other = nth(first, count, t)
            p = jnp.exp2(scores[t] * SCALE2 - (peak + pen(t, count)))
            total = total + (p[:, :HEAD] + p[:, HEAD:])
            acc = acc + dot(p.astype(BF16), kv[other, 1], NN)
        sums = jnp.sum(total, axis=1, keepdims=True)
        attended = (acc / sums).astype(BF16)
        out_send[k] = attended
        lse = peak + jnp.log2(sums)
        rd = jnp.sum(qd[sl, 1].astype(F32) * attended.astype(F32), axis=1, keepdims=True)
        lse_col[k] = jnp.broadcast_to(lse, (TOK, HEAD))
        dot_col[k] = jnp.broadcast_to(rd, (TOK, HEAD))
        lane = lax.broadcasted_iota(jnp.int32, (TOK, HEAD), 1)
        turned = jnp.where(lane < 8, lse, rd).T
        stats[member, k] = turned[:16]

        @pl.when(k == 0)
        def _():
            out_home[head] = out_send[0]

        @pl.when(k > 0)
        def _():
            send_out(k).start()

        return carry

    lax.fori_loop(0, 4, forward_block, 0)

    quad = [
        other_core, near, at(z_=partner, core_=1 - core), other_row,
        at(1 - yh, z, 1 - core), at(1 - yh, partner, core), at(1 - yh, partner, 1 - core),
    ]

    def send_stats(i):
        return remote(stats.at[member], stats.at[member], st_s.at[i], st_r.at[i], quad[i])

    for i in range(7):
        send_stats(i).start()

    def home_out(k):
        t = targets[k]
        return remote(out_send.at[k], out_home.at[t // 2], o_s.at[k], o_r.at[k], at(z_=t))

    def ar_core():
        return remote(wp.at[1 - core], rc, ar_s.at[4, 0, 0], ar_r.at[4, 0, 0], other_core)

    def step1(half, o):
        there = at_x(o) if half == 0 else at_y(o)
        mine = x if half == 0 else y
        return remote(
            wc.at[half, (mine + o) % 4], rx.at[half, o - 1], ar_s.at[0, half, o], ar_r.at[0, half, o], there
        )

    def step2(half, o):
        there = at_y(o) if half == 0 else at_x(o)
        mine = y if half == 0 else x
        return remote(
            wx.at[half, (mine + o) % 4], rxy.at[half, o - 1], ar_s.at[1, half, o], ar_r.at[1, half, o], there
        )

    def ar_z(o):
        t = (z + o) % 8
        return remote(wz.at[t], rz.at[o - 1], az_s.at[0, o], az_r.at[0, o], at(z_=t))

    def back_z(o):
        return remote(fz.at[z], fz.at[z], az_s.at[1, o], az_r.at[1, o], at(z_=(z + o) % 8))

    firsts, seconds = (x, y), (y, x)

    def final_row(half):
        return pl.multiple_of(firsts[half] * 64 + seconds[half] * 16, 16)

    def back2(half, o):
        part = gwf.at[core, half, pl.ds(final_row(half), 16)]
        there = at_y(o) if half == 0 else at_x(o)
        return remote(part, part, ar_s.at[2, half, o], ar_r.at[2, half, o], there)

    def back1(half, o):
        part = gwf.at[core, half, pl.ds(pl.multiple_of(firsts[half] * 64, 64), 64)]
        there = at_x(o) if half == 0 else at_y(o)
        return remote(part, part, ar_s.at[3, half, o], ar_r.at[3, half, o], there)

    def back_core(half, o):
        piece = (firsts[half] - o + 4) % 4
        part = gwf.at[core, half, pl.ds(pl.multiple_of(piece * 64, 64), 64)]
        return remote(part, part, wb_s.at[half, o], wb_r.at[half, o], other_core)

    def weight_term():
        for k in (1, 2, 3):
            home_out(k).wait_recv()
        for c in (1 - core, core):
            for i in range(2):
                part = dot(out_home[2 * c + i], cot_ref[...], TN).astype(BF16)
                for half in range(2):
                    for a in range(2):
                        for b in range(4):
                            rows = slice(a * 64 + b * 16, a * 64 + b * 16 + 16)
                            wp[c, half, i * 2 + a, b] = part[rows, half * 512 : half * 512 + 512]
            if c is not core:
                ar_core().start()

    def sum_core():
        ar_core().wait_recv()
        wc[...] = (wp[core].astype(F32) + rc[...].astype(F32)).astype(BF16)
        for o in (1, 2, 3):
            for half in range(2):
                step1(half, o).start()

    def sum_1():
        for half in range(2):
            total = wc[half, firsts[half]].astype(F32)
            for o in (1, 2, 3):
                step1(half, o).wait_recv()
                total = total + rx[half, o - 1].astype(F32)
            wx[half] = total.astype(BF16)
            for o in (1, 2, 3):
                step2(half, o).start()

    def sum_2():
        for half in range(2):
            total = wx[half, seconds[half]].astype(F32)
            for o in (1, 2, 3):
                step2(half, o).wait_recv()
                total = total + rxy[half, o - 1].astype(F32)
            total = total.astype(BF16)
            for j in range(4):
                wz[half * 4 + j] = total[:, j * HEAD : (j + 1) * HEAD]
        for o in range(1, 8):
            ar_z(o).start()

    def sum_z():
        total = wz[z].astype(F32)
        for o in range(1, 8):
            ar_z(o).wait_recv()
            total = total + rz[o - 1].astype(F32)
        rows = TOK * lax.axis_size("ctx") * lax.axis_size("dp")
        fz[z] = (total * (1.0 / math.sqrt(rows))).astype(BF16)
        for o in range(1, 8):
            back_z(o).start()

    def gather_z():
        for o in range(1, 8):
            back_z(o).wait_recv()
        for half in range(2):
            for j in range(4):
                cols = slice(j * HEAD, (j + 1) * HEAD)
                gwf[core, half, pl.ds(final_row(half), 16), cols] = fz[half * 4 + j]
            for o in (1, 2, 3):
                back2(half, o).start()

    def gather_2():
        for half in range(2):
            for o in (1, 2, 3):
                back2(half, o).wait_recv()
            for o in (1, 2, 3):
                back1(half, o).start()
            back_core(half, 0).start()

    def gather_1():
        for half in range(2):
            for o in (1, 2, 3):
                back1(half, o).wait_recv()
                back_core(half, o).start()

    def send_grad(a, k):
        return remote(
            grad_send.at[a, k], grad_home.at[a, head], g_s.at[a, k], g_r.at[a, k], at(z_=own_z(k))
        )

    def give_grad(a, k, value):
        grad_send[a, k] = value

        @pl.when(k == 0)
        def _():
            grad_home[a, head] = grad_send[a, 0]

    def query_block(k, carry):
        @pl.when(k == 0)
        def _():
            for j in range(4):
                spread_their(1, j)

        @pl.when(k == 2)
        def _():
            weight_term()

        @pl.when(k == 3)
        def _():
            sum_core()

        sl = slot(own_z(k), core)
        first, count = block_range(k)
        query, grad = qd[sl, 0], qd[sl, 1]
        lse = lse_col[k][:, :1]
        rd = dot_col[k][:, :1]
        acc = jnp.zeros((TOK, HEAD), F32)
        for t in range(MOST):
            other = nth(first, count, t)
            keys = kv[other, 0]
            p = jnp.exp2(dot(query, keys, NT) * SCALE2 - (lse + pen(t, count)))
            ds = (p * (dot(grad, kv[other, 1], NT) - rd)).astype(BF16)
            acc = acc + dot(ds, keys, NN)
        give_grad(0, k, (acc * FACTOR).astype(BF16))

        @pl.when(k > 0)
        def _():
            send_grad(0, k).start()

        return carry

    lax.fori_loop(0, 4, query_block, 0)

    for m in range(CROSS):
        spread_cross(1, m)
    sum_1()
    all_here(1)
    for i in range(7):
        send_stats(i).wait_recv()

    def key_block(k, carry):
        @pl.when(k == 1)
        def _():
            sum_2()

        @pl.when(k == 2)
        def _():
            sum_z()
            for a in (1, 2):
                send_grad(a, 1).start()

        @pl.when(k == 3)
        def _():
            gather_z()

        sl = slot(own_z(k), core)
        first, count = block_range(k)
        keys, values = kv[sl, 0], kv[sl, 1]
        acc_k = jnp.zeros((TOK, HEAD), F32)
        acc_v = jnp.zeros((TOK, HEAD), F32)
        for t in range(MOST):
            other = nth(first, count, t)
            block = other + 6 * yh
            oz = (block // 2) % 8
            left = (2 * head - oz + 8) % 8
            in_left = left < 4
            k_of = jnp.where(in_left, left, 7 - left)
            who = (block // 16) * 4 + jnp.where(in_left, 0, 2) + block % 2
            lse = stats[who, k_of, 0:1, :]
            rd = stats[who, k_of, 8:9, :]
            query, grad = qd[other, 0], qd[other, 1]
            p = jnp.exp2(dot(keys, query, NT) * SCALE2 - (lse + pen(t, count)))
            acc_v = acc_v + dot(p.astype(BF16), grad, NN)
            ds = (p * (dot(values, grad, NT) - rd)).astype(BF16)
            acc_k = acc_k + dot(ds, query, NN)
        give_grad(1, k, (acc_k * FACTOR).astype(BF16))
        give_grad(2, k, acc_v.astype(BF16))

        @pl.when(k >= 2)
        def _():
            for a in (1, 2):
                send_grad(a, k).start()

        return carry

    lax.fori_loop(0, 4, key_block, 0)

    def home_grad(a, k):
        t = targets[k]
        return remote(
            grad_send.at[a, k], grad_home.at[a, t // 2], g_s.at[a, k], g_r.at[a, k], at(z_=t)
        )

    stores = []

    def store(src, dst):
        copy = pltpu.make_async_copy(src, dst, out_s.at[len(stores)])
        copy.start()
        stores.append(copy)

    def finish(a, dst):
        for k in (1, 2, 3):
            home_grad(a, k).wait_recv()
        for h in range(HEADS):
            store(grad_home.at[a, h], dst.at[:, pl.ds(h * HEAD, HEAD)])

    gather_2()
    projected = dot(out_home[0], w_ref[0:HEAD], NN)
    for h in range(1, HEADS):
        projected = projected + dot(out_home[h], w_ref[h * HEAD : (h + 1) * HEAD], NN)
    proj_ref[...] = projected.astype(BF16)
    store(proj_ref, proj_hbm)
    finish(0, gq_hbm)
    gather_1()
    finish(1, gk_hbm)
    finish(2, gv_hbm)

    def store_weight(c):
        for half in range(2):
            rows, cols = pl.ds(pl.multiple_of(c * 256, 256), 256), pl.ds(half * 512, 512)
            store(gwf.at[c, half], gw_hbm.at[rows, cols])

    store_weight(core)
    for half in range(2):
        for o in range(4):
            back_core(half, o).wait_recv()
    store_weight(1 - core)
    for copy in stores:
        copy.wait()

    for k in (1, 2, 3):
        for kind in range(3):
            leg1(kind, k).wait_send()
        send_out(k).wait_send()
        for a in range(3):
            send_grad(a, k).wait_send()
    for g in range(2):
        for k in range(4):
            leg2(g, k).wait_send()
            core1(g, k).wait_send()
            core2(g, k).wait_send()
        for m in range(CROSS):
            leg3(g, m).wait_send()
            cross_core(g, m).wait_send()
    for i in range(7):
        send_stats(i).wait_send()
    ar_core().wait_send()
    for o in (1, 2, 3):
        for half in range(2):
            for make in (step1, step2, back2, back1):
                make(half, o).wait_send()
    for o in range(1, 8):
        ar_z(o).wait_send()
        back_z(o).wait_send()
    for half in range(2):
        for o in range(4):
            back_core(half, o).wait_send()


def hand_on(*refs):
    held, in_sems, out_sems = refs[10:15], refs[15], refs[16]
    copies = []
    for src, dst, mid in zip(refs[:5], refs[5:10], held):
        rows = src.shape[0] // 2
        for part in range(2):
            piece, i = pl.ds(part * rows, rows), len(copies)
            copies.append(
                (
                    pltpu.make_async_copy(src.at[piece], mid.at[piece], in_sems.at[i]),
                    pltpu.make_async_copy(mid.at[piece], dst.at[piece], out_sems.at[i]),
                )
            )
    for come, _ in copies:
        come.start()
    for come, go in copies:
        come.wait()
        go.start()
    for _, go in copies:
        go.wait()


def on_device(query_rows, key_rows, value_rows, recordings, out_weight, cotangent):
    vmem = pltpu.VMEM
    smem = pl.BlockSpec(memory_space=pltpu.SMEM)
    hbm = pl.BlockSpec(memory_space=pl.ANY)
    dma = pltpu.SemaphoreType.DMA
    shapes = [(TOK, D), (TOK, ATT), (TOK, ATT), (TOK, ATT), (ATT, D)]
    shapes = tuple(jax.ShapeDtypeStruct(shape, BF16) for shape in shapes)
    results = pl.pallas_call(
        kernel,
        out_shape=shapes,
        in_specs=[smem, hbm, hbm, hbm, hbm, hbm],
        out_specs=(hbm,) * 5,
        scratch_shapes=[
            vmem((TOK, D), BF16),
            vmem((ATT, D), BF16),
            vmem((TOK, D), BF16),
            pltpu.SMEM((2, 4), jnp.int32),
            vmem((WINDOW, 2, TOK, HEAD), BF16),
            vmem((WINDOW, 2, TOK, HEAD), BF16),
            vmem((HEADS, 2, TOK, HEAD), BF16),
            vmem((HEADS, TOK, HEAD), BF16),
            vmem((HEADS, TOK, HEAD), BF16),
            vmem((8, 4, 16, TOK), F32),
            vmem((4, TOK, HEAD), F32),
            vmem((4, TOK, HEAD), F32),
            vmem((MOST, TOK, TOK), F32),
            vmem((4, TOK, HEAD), BF16),
            vmem((HEADS, TOK, HEAD), BF16),
            vmem((3, 4, TOK, HEAD), BF16),
            vmem((3, HEADS, TOK, HEAD), BF16),
            vmem((2, 2, 4, 4, 16, 512), BF16),
            vmem((2, 4, 4, 16, 512), BF16),
            vmem((2, 4, 4, 16, 512), BF16),
            vmem((2, 4, 16, 512), BF16),
            vmem((2, 3, 4, 16, 512), BF16),
            vmem((2, 3, 16, 512), BF16),
            vmem((8, 16, HEAD), BF16),
            vmem((7, 16, HEAD), BF16),
            vmem((8, 16, HEAD), BF16),
            vmem((2, 2, 256, 512), BF16),
        ]
        + [dma((3, 4))] * 2
        + [dma((2, 4))] * 6
        + [dma((2, CROSS))] * 4
        + [dma((7,))] * 2
        + [dma((4,))] * 2
        + [dma((3, 4))] * 2
        + [dma((5, 2, 4))] * 2
        + [dma((2, 8))] * 2
        + [dma((2, 4))] * 2
        + [dma((14,)), dma((17,))],
        compiler_params=pltpu.CompilerParams(
            collective_id=0, has_side_effects=True, vmem_limit_bytes=56 << 20
        ),
    )(recordings, query_rows[0], key_rows[0], value_rows[0], cotangent[0], out_weight)
    projected, grad_query, grad_key, grad_value, grad_weight = pl.pallas_call(
        hand_on,
        out_shape=shapes,
        in_specs=[hbm] * 5,
        out_specs=(hbm,) * 5,
        scratch_shapes=[vmem(shape.shape, BF16) for shape in shapes] + [dma((10,))] * 2,
    )(*results)
    return (projected[None], grad_query[None], grad_key[None], grad_value[None], grad_weight)


def solution(mesh):
    rows = P("dp", "ctx", None)
    return jax.shard_map(
        on_device,
        mesh=mesh,
        in_specs=(rows, rows, rows, P("dp", None), P(), rows),
        out_specs=(rows, rows, rows, rows, P()),
        check_vma=False,
    )
```

```python
import functools
import math

import jax
import jax.numpy as jnp
from jax import lax
from jax.experimental import pallas as pl
from jax.experimental.pallas import tpu as pltpu
from jax.sharding import PartitionSpec as P

HEADS = 4
HEAD = 128
MOST = 11
TOK = 256
D = 1024
ATT = 512
BLOCKS = 32
WINDOW = 26
CROSS = 5
FACTOR = 1.0 / math.sqrt(HEAD)
SCALE2 = FACTOR * math.log2(math.e)
FAR = 1e30
MESH = pl.DeviceIdType.MESH
F32 = jnp.float32
BF16 = jnp.bfloat16


def dot(a, b, dims):
    return lax.dot_general(a, b, (dims, ((), ())), preferred_element_type=F32)


NT = ((1,), (1,))
NN = ((1,), (0,))
TN = ((0,), (0,))


def kernel(
    rec_ref, q_hbm, k_hbm, v_hbm, cot_hbm, w_hbm,
    proj_hbm, gq_hbm, gk_hbm, gv_hbm, gw_hbm,
    cot_ref, w_ref, proj_ref, ranges,
    kv, qd, pack_kv, pack_q, pack_d, stats, lse_col, dot_col, scores,
    out_send, out_home, grad_send, grad_home,
    wp, wc, rc, wx, rx, rxy, wz, rz, fz, gwf,
    s1_s, s1_r, s2_s, s2_r, c1_s, c1_r, c2_s, c2_r, s3_s, s3_r, cx_s, cx_r,
    st_s, st_r, o_s, o_r, g_s, g_r, ar_s, ar_r, az_s, az_r, wb_s, wb_r, in_s, out_s,
):
    ctx = lax.axis_index("ctx")
    dp = lax.axis_index("dp")
    yh, z, core = ctx // 16, (ctx // 2) % 8, ctx % 2
    yl, x = dp // 4, dp % 4
    y = yh * 2 + yl
    side = 2 * (z % 2) - 1
    head = z // 2
    partner = (z - side + 8) % 8

    def at(yh_=None, z_=None, core_=None):
        a = yh if yh_ is None else yh_
        b = z if z_ is None else z_
        c = core if core_ is None else core_
        return (a * 16 + b * 2 + c, dp)

    def at_x(o):
        return (ctx, yl * 4 + (x + o) % 4)

    def at_y(o):
        y2 = (y + o) % 4
        return ((y2 // 2) * 16 + z * 2 + core, (y2 % 2) * 4 + x)

    other_core = at(core_=1 - core)
    other_row = at(yh_=1 - yh)
    near = at(z_=partner)

    def own_z(k):
        return (z + side * k + 8) % 8

    def their_z(k):
        return (z - side * (k + 1) + 8) % 8

    def slot(zz, cc):
        return 10 * yh + 2 * zz + cc

    targets = [None, (z + side + 8) % 8, (z - 2 * side + 8) % 8, (z + 3 * side + 8) % 8]

    def remote(src, dst, ss, rs, device):
        return pltpu.make_async_remote_copy(
            src_ref=src, dst_ref=dst, send_sem=ss, recv_sem=rs, device_id=device, device_id_type=MESH
        )

    loads = []
    for h in range(HEADS):
        cols = pl.ds(h * HEAD, HEAD)
        loads.append((k_hbm.at[:, cols], pack_kv.at[h, 0]))
        loads.append((v_hbm.at[:, cols], pack_kv.at[h, 1]))
        loads.append((q_hbm.at[:, cols], pack_q.at[h]))
    loads += [(cot_hbm, cot_ref), (w_hbm, w_ref)]
    loads = [pltpu.make_async_copy(src, dst, in_s.at[i]) for i, (src, dst) in enumerate(loads)]
    for load in loads:
        load.start()

    peers = [other_core, at(z_=partner, core_=1 - core)]
    peers += [at(z_=(z + o) % 8) for o in range(1, 8)]
    peers += [at_x(o) for o in range(1, 4)]
    peers += [at_y(o) for o in range(1, 4)]
    peers += [
        at(1 - yh, z, 1 - core),
        at(1 - yh, partner, core),
        at(1 - yh, partner, 1 - core),
    ]
    barrier = pltpu.get_barrier_semaphore()
    for peer in peers:
        pl.semaphore_signal(barrier, inc=1, device_id=peer, device_id_type=MESH)
    for k in range(4):
        label = rec_ref[0, 16 * yh + 2 * own_z(k) + core]
        first = jnp.int32(0)
        count = jnp.int32(0)
        for j in range(BLOCKS):
            first = first + jnp.where(rec_ref[0, j] < label, 1, 0)
            count = count + jnp.where(rec_ref[0, j] == label, 1, 0)
        ranges[0, k] = first - 6 * yh
        ranges[1, k] = count
    for load in loads[:12]:
        load.wait()
    pl.semaphore_wait(barrier, len(peers))

    home = slot(z, core)

    def leg1(kind, k):
        t = targets[k]
        if kind == 0:
            src, dst = pack_kv.at[t // 2], kv.at[home]
        elif kind == 1:
            src, dst = pack_q.at[t // 2], qd.at[home, 0]
        else:
            src, dst = pack_d.at[t // 2], qd.at[home, 1]
        return remote(src, dst, s1_s.at[kind, k], s1_r.at[kind, k], at(z_=t))

    for kind in (0, 1):
        for k in (1, 2, 3):
            leg1(kind, k).start()
    kv[home] = pack_kv[head]
    qd[home, 0] = pack_q[head]

    bufs = (kv, qd)

    def leg2(g, k):
        sl = slot(own_z(k), core)
        return remote(bufs[g].at[sl], bufs[g].at[sl], s2_s.at[g, k], s2_r.at[g, k], near)

    def core1(g, k):
        sl = slot(own_z(k), core)
        return remote(bufs[g].at[sl], bufs[g].at[sl], c1_s.at[g, k], c1_r.at[g, k], other_core)

    def core2(g, k):
        sl = slot(their_z(k), core)
        return remote(bufs[g].at[sl], bufs[g].at[sl], c2_s.at[g, k], c2_r.at[g, k], other_core)

    def leg3(g, m):
        src = slot(m + 3 * (1 - yh), core)
        dst = 2 * m + core + 16 * yh
        return remote(bufs[g].at[src], bufs[g].at[dst], s3_s.at[g, m], s3_r.at[g, m], other_row)

    def cross_core(g, m):
        sl = 2 * m + core + 16 * (1 - yh)
        return remote(bufs[g].at[sl], bufs[g].at[sl], cx_s.at[g, m], cx_r.at[g, m], other_core)

    def maybe_leg3(g, zz):
        m = zz - 3 * (1 - yh)

        @pl.when(jnp.logical_and(m >= 0, m < CROSS))
        def _():
            leg3(g, m).start()

    def spread_row(g, k):
        leg2(g, k).start()
        core1(g, k).start()

    def spread_own(g, k):
        spread_row(g, k)
        maybe_leg3(g, own_z(k))

    def spread_their(g, k):
        leg2(g, k).wait_recv()
        maybe_leg3(g, their_z(k))
        core2(g, k).start()

    def spread_cross(g, m):
        leg3(g, m).wait_recv()
        cross_core(g, m).start()

    def all_here(g):
        for k in range(4):
            core1(g, k).wait_recv()
            core2(g, k).wait_recv()
        for m in range(CROSS):
            cross_core(g, m).wait_recv()

    spread_own(0, 0)
    for load in loads[12:]:
        load.wait()
    grad_att = dot(cot_ref[...], w_ref[...], NT).astype(BF16)
    for h in range(HEADS):
        pack_d[h] = grad_att[:, h * HEAD : (h + 1) * HEAD]
    qd[home, 1] = pack_d[head]
    for k in (1, 2, 3):
        leg1(2, k).start()
    for k in (1, 2, 3):
        leg1(0, k).wait_recv()
        spread_own(0, k)
    for k in range(4):
        spread_their(0, k)
    spread_row(1, 0)
    for k in (1, 2, 3):
        leg1(1, k).wait_recv()
        leg1(2, k).wait_recv()
        spread_row(1, k)
    for m in range(CROSS):
        spread_cross(0, m)
    for k in range(4):
        maybe_leg3(1, own_z(k))
    all_here(0)

    member = yh * 4 + (z % 2) * 2 + core

    def send_out(k):
        return remote(out_send.at[k], out_home.at[head], o_s.at[k], o_r.at[k], at(z_=own_z(k)))

    def block_range(k):
        return ranges[0, k], ranges[1, k]

    def nth(first, count, t):
        return jnp.clip(first + jnp.minimum(t, count - 1), 0, WINDOW - 1)

    def pen(t, count):
        return jnp.where(t < count, 0.0, FAR)

    def forward_block(k, carry):
        @pl.when(k == 3)
        def _():
            for j in range(4):
                spread_their(1, j)

        sl = slot(own_z(k), core)
        first, count = block_range(k)
        query = qd[sl, 0]
        top = None
        for t in range(MOST):
            other = nth(first, count, t)
            s = dot(query, kv[other, 0], NT)
            scores[t] = s
            top = s if top is None else jnp.maximum(top, s)
        peak = jnp.max(top, axis=1, keepdims=True) * SCALE2
        total = jnp.zeros((TOK, HEAD), F32)
        acc = jnp.zeros((TOK, HEAD), F32)
        for t in range(MOST):
            other = nth(first, count, t)
            p = jnp.exp2(scores[t] * SCALE2 - (peak + pen(t, count)))
            total = total + (p[:, :HEAD] + p[:, HEAD:])
            acc = acc + dot(p.astype(BF16), kv[other, 1], NN)
        sums = jnp.sum(total, axis=1, keepdims=True)
        attended = (acc / sums).astype(BF16)
        out_send[k] = attended
        lse = peak + jnp.log2(sums)
        rd = jnp.sum(qd[sl, 1].astype(F32) * attended.astype(F32), axis=1, keepdims=True)
        lse_col[k] = jnp.broadcast_to(lse, (TOK, HEAD))
        dot_col[k] = jnp.broadcast_to(rd, (TOK, HEAD))
        lane = lax.broadcasted_iota(jnp.int32, (TOK, HEAD), 1)
        turned = jnp.where(lane < 8, lse, rd).T
        stats[member, k] = turned[:16]

        @pl.when(k == 0)
        def _():
            out_home[head] = out_send[0]

        @pl.when(k > 0)
        def _():
            send_out(k).start()

        return carry

    lax.fori_loop(0, 4, forward_block, 0)

    quad = [
        other_core, near, at(z_=partner, core_=1 - core), other_row,
        at(1 - yh, z, 1 - core), at(1 - yh, partner, core), at(1 - yh, partner, 1 - core),
    ]

    def send_stats(i):
        return remote(stats.at[member], stats.at[member], st_s.at[i], st_r.at[i], quad[i])

    for i in range(7):
        send_stats(i).start()

    def home_out(k):
        t = targets[k]
        return remote(out_send.at[k], out_home.at[t // 2], o_s.at[k], o_r.at[k], at(z_=t))

    def ar_core():
        return remote(wp.at[1 - core], rc, ar_s.at[4, 0, 0], ar_r.at[4, 0, 0], other_core)

    def step1(half, o):
        there = at_x(o) if half == 0 else at_y(o)
        mine = x if half == 0 else y
        return remote(
            wc.at[half, (mine + o) % 4], rx.at[half, o - 1], ar_s.at[0, half, o], ar_r.at[0, half, o], there
        )

    def step2(half, o):
        there = at_y(o) if half == 0 else at_x(o)
        mine = y if half == 0 else x
        return remote(
            wx.at[half, (mine + o) % 4], rxy.at[half, o - 1], ar_s.at[1, half, o], ar_r.at[1, half, o], there
        )

    def ar_z(o):
        t = (z + o) % 8
        return remote(wz.at[t], rz.at[o - 1], az_s.at[0, o], az_r.at[0, o], at(z_=t))

    def back_z(o):
        return remote(fz.at[z], fz.at[z], az_s.at[1, o], az_r.at[1, o], at(z_=(z + o) % 8))

    firsts, seconds = (x, y), (y, x)

    def final_row(half):
        return pl.multiple_of(firsts[half] * 64 + seconds[half] * 16, 16)

    def back2(half, o):
        part = gwf.at[core, half, pl.ds(final_row(half), 16)]
        there = at_y(o) if half == 0 else at_x(o)
        return remote(part, part, ar_s.at[2, half, o], ar_r.at[2, half, o], there)

    def back1(half, o):
        part = gwf.at[core, half, pl.ds(pl.multiple_of(firsts[half] * 64, 64), 64)]
        there = at_x(o) if half == 0 else at_y(o)
        return remote(part, part, ar_s.at[3, half, o], ar_r.at[3, half, o], there)

    def back_core(half, o):
        piece = (firsts[half] - o + 4) % 4
        part = gwf.at[core, half, pl.ds(pl.multiple_of(piece * 64, 64), 64)]
        return remote(part, part, wb_s.at[half, o], wb_r.at[half, o], other_core)

    def weight_term():
        for k in (1, 2, 3):
            home_out(k).wait_recv()
        for c in (1 - core, core):
            for i in range(2):
                part = dot(out_home[2 * c + i], cot_ref[...], TN).astype(BF16)
                for half in range(2):
                    for a in range(2):
                        for b in range(4):
                            rows = slice(a * 64 + b * 16, a * 64 + b * 16 + 16)
                            wp[c, half, i * 2 + a, b] = part[rows, half * 512 : half * 512 + 512]
            if c is not core:
                ar_core().start()

    def sum_core():
        ar_core().wait_recv()
        wc[...] = (wp[core].astype(F32) + rc[...].astype(F32)).astype(BF16)
        for o in (1, 2, 3):
            for half in range(2):
                step1(half, o).start()

    def sum_1():
        for half in range(2):
            total = wc[half, firsts[half]].astype(F32)
            for o in (1, 2, 3):
                step1(half, o).wait_recv()
                total = total + rx[half, o - 1].astype(F32)
            wx[half] = total.astype(BF16)
            for o in (1, 2, 3):
                step2(half, o).start()

    def sum_2():
        for half in range(2):
            total = wx[half, seconds[half]].astype(F32)
            for o in (1, 2, 3):
                step2(half, o).wait_recv()
                total = total + rxy[half, o - 1].astype(F32)
            total = total.astype(BF16)
            for j in range(4):
                wz[half * 4 + j] = total[:, j * HEAD : (j + 1) * HEAD]
        for o in range(1, 8):
            ar_z(o).start()

    def sum_z():
        total = wz[z].astype(F32)
        for o in range(1, 8):
            ar_z(o).wait_recv()
            total = total + rz[o - 1].astype(F32)
        rows = TOK * lax.axis_size("ctx") * lax.axis_size("dp")
        fz[z] = (total * (1.0 / math.sqrt(rows))).astype(BF16)
        for o in range(1, 8):
            back_z(o).start()

    def gather_z():
        for o in range(1, 8):
            back_z(o).wait_recv()
        for half in range(2):
            for j in range(4):
                cols = slice(j * HEAD, (j + 1) * HEAD)
                gwf[core, half, pl.ds(final_row(half), 16), cols] = fz[half * 4 + j]
            for o in (1, 2, 3):
                back2(half, o).start()

    def gather_2():
        for half in range(2):
            for o in (1, 2, 3):
                back2(half, o).wait_recv()
            for o in (1, 2, 3):
                back1(half, o).start()
            back_core(half, 0).start()

    def gather_1():
        for half in range(2):
            for o in (1, 2, 3):
                back1(half, o).wait_recv()
                back_core(half, o).start()

    def send_grad(a, k):
        return remote(
            grad_send.at[a, k], grad_home.at[a, head], g_s.at[a, k], g_r.at[a, k], at(z_=own_z(k))
        )

    def give_grad(a, k, value):
        grad_send[a, k] = value

        @pl.when(k == 0)
        def _():
            grad_home[a, head] = grad_send[a, 0]

    def query_block(k, carry):
        @pl.when(k == 2)
        def _():
            weight_term()

        @pl.when(k == 3)
        def _():
            sum_core()

        sl = slot(own_z(k), core)
        first, count = block_range(k)
        query, grad = qd[sl, 0], qd[sl, 1]
        lse = lse_col[k][:, :1]
        rd = dot_col[k][:, :1]
        acc = jnp.zeros((TOK, HEAD), F32)
        for t in range(MOST):
            other = nth(first, count, t)
            keys = kv[other, 0]
            p = jnp.exp2(dot(query, keys, NT) * SCALE2 - (lse + pen(t, count)))
            ds = (p * (dot(grad, kv[other, 1], NT) - rd)).astype(BF16)
            acc = acc + dot(ds, keys, NN)
        give_grad(0, k, (acc * FACTOR).astype(BF16))

        @pl.when(k > 0)
        def _():
            send_grad(0, k).start()

        return carry

    lax.fori_loop(0, 4, query_block, 0)

    sum_1()
    for m in range(CROSS):
        spread_cross(1, m)
    all_here(1)
    sum_2()
    for i in range(7):
        send_stats(i).wait_recv()

    def key_block(k, carry):
        @pl.when(k == 1)
        def _():
            sum_z()

        @pl.when(k == 2)
        def _():
            gather_z()

        sl = slot(own_z(k), core)
        first, count = block_range(k)
        keys, values = kv[sl, 0], kv[sl, 1]
        acc_k = jnp.zeros((TOK, HEAD), F32)
        acc_v = jnp.zeros((TOK, HEAD), F32)
        for t in range(MOST):
            other = nth(first, count, t)
            block = other + 6 * yh
            oz = (block // 2) % 8
            left = (2 * head - oz + 8) % 8
            in_left = left < 4
            k_of = jnp.where(in_left, left, 7 - left)
            who = (block // 16) * 4 + jnp.where(in_left, 0, 2) + block % 2
            lse = stats[who, k_of, 0:1, :]
            rd = stats[who, k_of, 8:9, :]
            query, grad = qd[other, 0], qd[other, 1]
            p = jnp.exp2(dot(keys, query, NT) * SCALE2 - (lse + pen(t, count)))
            acc_v = acc_v + dot(p.astype(BF16), grad, NN)
            ds = (p * (dot(values, grad, NT) - rd)).astype(BF16)
            acc_k = acc_k + dot(ds, query, NN)
        give_grad(1, k, (acc_k * FACTOR).astype(BF16))
        give_grad(2, k, acc_v.astype(BF16))

        @pl.when(k >= 1)
        def _():
            for a in (1, 2):
                send_grad(a, k).start()

        return carry

    lax.fori_loop(0, 4, key_block, 0)

    def home_grad(a, k):
        t = targets[k]
        return remote(
            grad_send.at[a, k], grad_home.at[a, t // 2], g_s.at[a, k], g_r.at[a, k], at(z_=t)
        )

    stores = []

    def store(src, dst):
        copy = pltpu.make_async_copy(src, dst, out_s.at[len(stores)])
        copy.start()
        stores.append(copy)

    def finish(a, dst):
        for k in (1, 2, 3):
            home_grad(a, k).wait_recv()
        for h in range(HEADS):
            store(grad_home.at[a, h], dst.at[:, pl.ds(h * HEAD, HEAD)])

    gather_2()
    projected = dot(out_home[0], w_ref[0:HEAD], NN)
    for h in range(1, HEADS):
        projected = projected + dot(out_home[h], w_ref[h * HEAD : (h + 1) * HEAD], NN)
    proj_ref[...] = projected.astype(BF16)
    store(proj_ref, proj_hbm)
    finish(0, gq_hbm)
    gather_1()
    finish(1, gk_hbm)
    finish(2, gv_hbm)

    def store_weight(c):
        for half in range(2):
            rows, cols = pl.ds(pl.multiple_of(c * 256, 256), 256), pl.ds(half * 512, 512)
            store(gwf.at[c, half], gw_hbm.at[rows, cols])

    store_weight(core)
    for half in range(2):
        for o in range(4):
            back_core(half, o).wait_recv()
    store_weight(1 - core)
    for copy in stores:
        copy.wait()

    for k in (1, 2, 3):
        for kind in range(3):
            leg1(kind, k).wait_send()
        send_out(k).wait_send()
        for a in range(3):
            send_grad(a, k).wait_send()
    for g in range(2):
        for k in range(4):
            leg2(g, k).wait_send()
            core1(g, k).wait_send()
            core2(g, k).wait_send()
        for m in range(CROSS):
            leg3(g, m).wait_send()
            cross_core(g, m).wait_send()
    for i in range(7):
        send_stats(i).wait_send()
    ar_core().wait_send()
    for o in (1, 2, 3):
        for half in range(2):
            for make in (step1, step2, back2, back1):
                make(half, o).wait_send()
    for o in range(1, 8):
        ar_z(o).wait_send()
        back_z(o).wait_send()
    for half in range(2):
        for o in range(4):
            back_core(half, o).wait_send()


def hand_on(*refs):
    held, in_sems, out_sems = refs[10:15], refs[15], refs[16]
    copies = []
    for src, dst, mid in zip(refs[:5], refs[5:10], held):
        rows = src.shape[0] // 2
        for part in range(2):
            piece, i = pl.ds(part * rows, rows), len(copies)
            copies.append(
                (
                    pltpu.make_async_copy(src.at[piece], mid.at[piece], in_sems.at[i]),
                    pltpu.make_async_copy(mid.at[piece], dst.at[piece], out_sems.at[i]),
                )
            )
    for come, _ in copies:
        come.start()
    for come, go in copies:
        come.wait()
        go.start()
    for _, go in copies:
        go.wait()


def on_device(query_rows, key_rows, value_rows, recordings, out_weight, cotangent):
    vmem = pltpu.VMEM
    smem = pl.BlockSpec(memory_space=pltpu.SMEM)
    hbm = pl.BlockSpec(memory_space=pl.ANY)
    dma = pltpu.SemaphoreType.DMA
    shapes = [(TOK, D), (TOK, ATT), (TOK, ATT), (TOK, ATT), (ATT, D)]
    shapes = tuple(jax.ShapeDtypeStruct(shape, BF16) for shape in shapes)
    results = pl.pallas_call(
        kernel,
        out_shape=shapes,
        in_specs=[smem, hbm, hbm, hbm, hbm, hbm],
        out_specs=(hbm,) * 5,
        scratch_shapes=[
            vmem((TOK, D), BF16),
            vmem((ATT, D), BF16),
            vmem((TOK, D), BF16),
            pltpu.SMEM((2, 4), jnp.int32),
            vmem((WINDOW, 2, TOK, HEAD), BF16),
            vmem((WINDOW, 2, TOK, HEAD), BF16),
            vmem((HEADS, 2, TOK, HEAD), BF16),
            vmem((HEADS, TOK, HEAD), BF16),
            vmem((HEADS, TOK, HEAD), BF16),
            vmem((8, 4, 16, TOK), F32),
            vmem((4, TOK, HEAD), F32),
            vmem((4, TOK, HEAD), F32),
            vmem((MOST, TOK, TOK), F32),
            vmem((4, TOK, HEAD), BF16),
            vmem((HEADS, TOK, HEAD), BF16),
            vmem((3, 4, TOK, HEAD), BF16),
            vmem((3, HEADS, TOK, HEAD), BF16),
            vmem((2, 2, 4, 4, 16, 512), BF16),
            vmem((2, 4, 4, 16, 512), BF16),
            vmem((2, 4, 4, 16, 512), BF16),
            vmem((2, 4, 16, 512), BF16),
            vmem((2, 3, 4, 16, 512), BF16),
            vmem((2, 3, 16, 512), BF16),
            vmem((8, 16, HEAD), BF16),
            vmem((7, 16, HEAD), BF16),
            vmem((8, 16, HEAD), BF16),
            vmem((2, 2, 256, 512), BF16),
        ]
        + [dma((3, 4))] * 2
        + [dma((2, 4))] * 6
        + [dma((2, CROSS))] * 4
        + [dma((7,))] * 2
        + [dma((4,))] * 2
        + [dma((3, 4))] * 2
        + [dma((5, 2, 4))] * 2
        + [dma((2, 8))] * 2
        + [dma((2, 4))] * 2
        + [dma((14,)), dma((17,))],
        compiler_params=pltpu.CompilerParams(
            collective_id=0, has_side_effects=True, vmem_limit_bytes=56 << 20
        ),
    )(recordings, query_rows[0], key_rows[0], value_rows[0], cotangent[0], out_weight)
    projected, grad_query, grad_key, grad_value, grad_weight = pl.pallas_call(
        hand_on,
        out_shape=shapes,
        in_specs=[hbm] * 5,
        out_specs=(hbm,) * 5,
        scratch_shapes=[vmem(shape.shape, BF16) for shape in shapes] + [dma((10,))] * 2,
    )(*results)
    return (projected[None], grad_query[None], grad_key[None], grad_value[None], grad_weight)


def solution(mesh):
    rows = P("dp", "ctx", None)
    return jax.shard_map(
        on_device,
        mesh=mesh,
        in_specs=(rows, rows, rows, P("dp", None), P(), rows),
        out_specs=(rows, rows, rows, rows, P()),
        check_vma=False,
    )
```

```python
import functools
import math

import jax
import jax.numpy as jnp
from jax import lax
from jax.experimental import pallas as pl
from jax.experimental.pallas import tpu as pltpu
from jax.sharding import PartitionSpec as P

HEADS = 4
HEAD = 128
MOST = 11
TOK = 256
D = 1024
ATT = 512
BLOCKS = 32
WINDOW = 26
CROSS = 5
FACTOR = 1.0 / math.sqrt(HEAD)
SCALE2 = FACTOR * math.log2(math.e)
FAR = 1e30
MESH = pl.DeviceIdType.MESH
F32 = jnp.float32
BF16 = jnp.bfloat16


def dot(a, b, dims):
    return lax.dot_general(a, b, (dims, ((), ())), preferred_element_type=F32)


NT = ((1,), (1,))
NN = ((1,), (0,))
TN = ((0,), (0,))


def kernel(
    rec_ref, q_hbm, k_hbm, v_hbm, cot_hbm, w_hbm,
    proj_hbm, gq_hbm, gk_hbm, gv_hbm, gw_hbm,
    cot_ref, w_ref, proj_ref, ranges,
    kv, qd, pack_kv, pack_q, pack_d, stats, lse_col, dot_col, scores,
    out_send, out_home, grad_send, grad_home,
    wp, wc, rc, wx, rx, rxy, wz, rz, fz, gwf,
    s1_s, s1_r, s2_s, s2_r, c1_s, c1_r, c2_s, c2_r, s3_s, s3_r, cx_s, cx_r,
    st_s, st_r, o_s, o_r, g_s, g_r, ar_s, ar_r, az_s, az_r, wb_s, wb_r, in_s, out_s,
):
    ctx = lax.axis_index("ctx")
    dp = lax.axis_index("dp")
    yh, z, core = ctx // 16, (ctx // 2) % 8, ctx % 2
    yl, x = dp // 4, dp % 4
    y = yh * 2 + yl
    side = 2 * (z % 2) - 1
    head = z // 2
    partner = (z - side + 8) % 8

    def at(yh_=None, z_=None, core_=None):
        a = yh if yh_ is None else yh_
        b = z if z_ is None else z_
        c = core if core_ is None else core_
        return (a * 16 + b * 2 + c, dp)

    def at_x(o):
        return (ctx, yl * 4 + (x + o) % 4)

    def at_y(o):
        y2 = (y + o) % 4
        return ((y2 // 2) * 16 + z * 2 + core, (y2 % 2) * 4 + x)

    other_core = at(core_=1 - core)
    other_row = at(yh_=1 - yh)
    near = at(z_=partner)

    def own_z(k):
        return (z + side * k + 8) % 8

    def their_z(k):
        return (z - side * (k + 1) + 8) % 8

    def slot(zz, cc):
        return 10 * yh + 2 * zz + cc

    targets = [None, (z + side + 8) % 8, (z - 2 * side + 8) % 8, (z + 3 * side + 8) % 8]

    def remote(src, dst, ss, rs, device):
        return pltpu.make_async_remote_copy(
            src_ref=src, dst_ref=dst, send_sem=ss, recv_sem=rs, device_id=device, device_id_type=MESH
        )

    loads = []
    for h in range(HEADS):
        cols = pl.ds(h * HEAD, HEAD)
        loads.append((k_hbm.at[:, cols], pack_kv.at[h, 0]))
        loads.append((v_hbm.at[:, cols], pack_kv.at[h, 1]))
        loads.append((q_hbm.at[:, cols], pack_q.at[h]))
    loads += [(cot_hbm, cot_ref), (w_hbm, w_ref)]
    loads = [pltpu.make_async_copy(src, dst, in_s.at[i]) for i, (src, dst) in enumerate(loads)]
    for load in loads:
        load.start()

    peers = [other_core, at(z_=partner, core_=1 - core)]
    peers += [at(z_=(z + o) % 8) for o in range(1, 8)]
    peers += [at_x(o) for o in range(1, 4)]
    peers += [at_y(o) for o in range(1, 4)]
    peers += [
        at(1 - yh, z, 1 - core),
        at(1 - yh, partner, core),
        at(1 - yh, partner, 1 - core),
    ]
    barrier = pltpu.get_barrier_semaphore()
    for peer in peers:
        pl.semaphore_signal(barrier, inc=1, device_id=peer, device_id_type=MESH)
    for k in range(4):
        label = rec_ref[0, 16 * yh + 2 * own_z(k) + core]
        first = jnp.int32(0)
        count = jnp.int32(0)
        for j in range(BLOCKS):
            first = first + jnp.where(rec_ref[0, j] < label, 1, 0)
            count = count + jnp.where(rec_ref[0, j] == label, 1, 0)
        ranges[0, k] = first - 6 * yh
        ranges[1, k] = count
    for load in loads[:12]:
        load.wait()
    pl.semaphore_wait(barrier, len(peers))

    home = slot(z, core)

    def leg1(kind, k):
        t = targets[k]
        if kind == 0:
            src, dst = pack_kv.at[t // 2], kv.at[home]
        elif kind == 1:
            src, dst = pack_q.at[t // 2], qd.at[home, 0]
        else:
            src, dst = pack_d.at[t // 2], qd.at[home, 1]
        return remote(src, dst, s1_s.at[kind, k], s1_r.at[kind, k], at(z_=t))

    for kind in (0, 1):
        for k in (1, 2, 3):
            leg1(kind, k).start()
    kv[home] = pack_kv[head]
    qd[home, 0] = pack_q[head]

    bufs = (kv, qd)

    def leg2(g, k):
        sl = slot(own_z(k), core)
        return remote(bufs[g].at[sl], bufs[g].at[sl], s2_s.at[g, k], s2_r.at[g, k], near)

    def core1(g, k):
        sl = slot(own_z(k), core)
        return remote(bufs[g].at[sl], bufs[g].at[sl], c1_s.at[g, k], c1_r.at[g, k], other_core)

    def core2(g, k):
        sl = slot(their_z(k), core)
        return remote(bufs[g].at[sl], bufs[g].at[sl], c2_s.at[g, k], c2_r.at[g, k], other_core)

    def leg3(g, m):
        src = slot(m + 3 * (1 - yh), core)
        dst = 2 * m + core + 16 * yh
        return remote(bufs[g].at[src], bufs[g].at[dst], s3_s.at[g, m], s3_r.at[g, m], other_row)

    def cross_core(g, m):
        sl = 2 * m + core + 16 * (1 - yh)
        return remote(bufs[g].at[sl], bufs[g].at[sl], cx_s.at[g, m], cx_r.at[g, m], other_core)

    def maybe_leg3(g, zz):
        m = zz - 3 * (1 - yh)

        @pl.when(jnp.logical_and(m >= 0, m < CROSS))
        def _():
            leg3(g, m).start()

    def spread_row(g, k):
        leg2(g, k).start()
        core1(g, k).start()

    def spread_own(g, k):
        spread_row(g, k)
        maybe_leg3(g, own_z(k))

    def spread_their(g, k):
        leg2(g, k).wait_recv()
        maybe_leg3(g, their_z(k))
        core2(g, k).start()

    def spread_cross(g, m):
        leg3(g, m).wait_recv()
        cross_core(g, m).start()

    def all_here(g):
        for k in range(4):
            core1(g, k).wait_recv()
            core2(g, k).wait_recv()
        for m in range(CROSS):
            cross_core(g, m).wait_recv()

    spread_own(0, 0)
    for load in loads[12:]:
        load.wait()
    grad_att = dot(cot_ref[...], w_ref[...], NT).astype(BF16)
    for h in range(HEADS):
        pack_d[h] = grad_att[:, h * HEAD : (h + 1) * HEAD]
    qd[home, 1] = pack_d[head]
    for k in (1, 2, 3):
        leg1(2, k).start()
    for k in (1, 2, 3):
        leg1(0, k).wait_recv()
        spread_own(0, k)
    for k in range(4):
        spread_their(0, k)
    spread_row(1, 0)
    for k in (1, 2, 3):
        leg1(1, k).wait_recv()
        leg1(2, k).wait_recv()
        spread_row(1, k)
    for m in range(CROSS):
        spread_cross(0, m)
    for k in range(4):
        maybe_leg3(1, own_z(k))
    all_here(0)

    member = yh * 4 + (z % 2) * 2 + core

    def send_out(k):
        return remote(out_send.at[k], out_home.at[head], o_s.at[k], o_r.at[k], at(z_=own_z(k)))

    def block_range(k):
        return ranges[0, k], ranges[1, k]

    def nth(first, count, t):
        return jnp.clip(first + jnp.minimum(t, count - 1), 0, WINDOW - 1)

    def pen(t, count):
        return jnp.where(t < count, 0.0, FAR)

    def forward_block(k, carry):
        @pl.when(k == 3)
        def _():
            for j in range(4):
                spread_their(1, j)

        sl = slot(own_z(k), core)
        first, count = block_range(k)
        query = qd[sl, 0]
        top = None
        for t in range(MOST):
            other = nth(first, count, t)
            s = dot(query, kv[other, 0], NT)
            scores[t] = s
            top = s if top is None else jnp.maximum(top, s)
        peak = jnp.max(top, axis=1, keepdims=True) * SCALE2
        total = jnp.zeros((TOK, HEAD), F32)
        acc = jnp.zeros((TOK, HEAD), F32)
        for t in range(MOST):
            other = nth(first, count, t)
            p = jnp.exp2(scores[t] * SCALE2 - (peak + pen(t, count)))
            total = total + (p[:, :HEAD] + p[:, HEAD:])
            acc = acc + dot(p.astype(BF16), kv[other, 1], NN)
        sums = jnp.sum(total, axis=1, keepdims=True)
        attended = (acc / sums).astype(BF16)
        out_send[k] = attended
        lse = peak + jnp.log2(sums)
        rd = jnp.sum(qd[sl, 1].astype(F32) * attended.astype(F32), axis=1, keepdims=True)
        lse_col[k] = jnp.broadcast_to(lse, (TOK, HEAD))
        dot_col[k] = jnp.broadcast_to(rd, (TOK, HEAD))
        lane = lax.broadcasted_iota(jnp.int32, (TOK, HEAD), 1)
        turned = jnp.where(lane < 8, lse, rd).T
        stats[member, k] = turned[:16]

        @pl.when(k == 0)
        def _():
            out_home[head] = out_send[0]

        @pl.when(k > 0)
        def _():
            send_out(k).start()

        return carry

    lax.fori_loop(0, 4, forward_block, 0)

    quad = [
        other_core, near, at(z_=partner, core_=1 - core), other_row,
        at(1 - yh, z, 1 - core), at(1 - yh, partner, core), at(1 - yh, partner, 1 - core),
    ]

    def send_stats(i):
        return remote(stats.at[member], stats.at[member], st_s.at[i], st_r.at[i], quad[i])

    for i in range(7):
        send_stats(i).start()

    def home_out(k):
        t = targets[k]
        return remote(out_send.at[k], out_home.at[t // 2], o_s.at[k], o_r.at[k], at(z_=t))

    def ar_core():
        return remote(wp.at[1 - core], rc, ar_s.at[4, 0, 0], ar_r.at[4, 0, 0], other_core)

    def step1(half, o):
        there = at_x(o) if half == 0 else at_y(o)
        mine = x if half == 0 else y
        return remote(
            wc.at[half, (mine + o) % 4], rx.at[half, o - 1], ar_s.at[0, half, o], ar_r.at[0, half, o], there
        )

    def step2(half, o):
        there = at_y(o) if half == 0 else at_x(o)
        mine = y if half == 0 else x
        return remote(
            wx.at[half, (mine + o) % 4], rxy.at[half, o - 1], ar_s.at[1, half, o], ar_r.at[1, half, o], there
        )

    def ar_z(o):
        t = (z + o) % 8
        return remote(wz.at[t], rz.at[o - 1], az_s.at[0, o], az_r.at[0, o], at(z_=t))

    def back_z(o):
        return remote(fz.at[z], fz.at[z], az_s.at[1, o], az_r.at[1, o], at(z_=(z + o) % 8))

    firsts, seconds = (x, y), (y, x)

    def final_row(half):
        return pl.multiple_of(firsts[half] * 64 + seconds[half] * 16, 16)

    def back2(half, o):
        part = gwf.at[core, half, pl.ds(final_row(half), 16)]
        there = at_y(o) if half == 0 else at_x(o)
        return remote(part, part, ar_s.at[2, half, o], ar_r.at[2, half, o], there)

    def back1(half, o):
        part = gwf.at[core, half, pl.ds(pl.multiple_of(firsts[half] * 64, 64), 64)]
        there = at_x(o) if half == 0 else at_y(o)
        return remote(part, part, ar_s.at[3, half, o], ar_r.at[3, half, o], there)

    def back_core(half, o):
        piece = (firsts[half] - o + 4) % 4
        part = gwf.at[core, half, pl.ds(pl.multiple_of(piece * 64, 64), 64)]
        return remote(part, part, wb_s.at[half, o], wb_r.at[half, o], other_core)

    def weight_term():
        for k in (1, 2, 3):
            home_out(k).wait_recv()
        for c in (1 - core, core):
            for i in range(2):
                part = dot(out_home[2 * c + i], cot_ref[...], TN).astype(BF16)
                for half in range(2):
                    for a in range(2):
                        for b in range(4):
                            rows = slice(a * 64 + b * 16, a * 64 + b * 16 + 16)
                            wp[c, half, i * 2 + a, b] = part[rows, half * 512 : half * 512 + 512]
            if c is not core:
                ar_core().start()

    def sum_core():
        ar_core().wait_recv()
        wc[...] = (wp[core].astype(F32) + rc[...].astype(F32)).astype(BF16)
        for o in (1, 2, 3):
            for half in range(2):
                step1(half, o).start()

    def sum_1():
        for half in range(2):
            total = wc[half, firsts[half]].astype(F32)
            for o in (1, 2, 3):
                step1(half, o).wait_recv()
                total = total + rx[half, o - 1].astype(F32)
            wx[half] = total.astype(BF16)
            for o in (1, 2, 3):
                step2(half, o).start()

    def sum_2():
        for half in range(2):
            total = wx[half, seconds[half]].astype(F32)
            for o in (1, 2, 3):
                step2(half, o).wait_recv()
                total = total + rxy[half, o - 1].astype(F32)
            total = total.astype(BF16)
            for j in range(4):
                wz[half * 4 + j] = total[:, j * HEAD : (j + 1) * HEAD]
        for o in range(1, 8):
            ar_z(o).start()

    def sum_z():
        total = wz[z].astype(F32)
        for o in range(1, 8):
            ar_z(o).wait_recv()
            total = total + rz[o - 1].astype(F32)
        rows = TOK * lax.axis_size("ctx") * lax.axis_size("dp")
        fz[z] = (total * (1.0 / math.sqrt(rows))).astype(BF16)
        for o in range(1, 8):
            back_z(o).start()

    def gather_z():
        for o in range(1, 8):
            back_z(o).wait_recv()
        for half in range(2):
            for j in range(4):
                cols = slice(j * HEAD, (j + 1) * HEAD)
                gwf[core, half, pl.ds(final_row(half), 16), cols] = fz[half * 4 + j]
            for o in (1, 2, 3):
                back2(half, o).start()

    def gather_2():
        for half in range(2):
            for o in (1, 2, 3):
                back2(half, o).wait_recv()
            for o in (1, 2, 3):
                back1(half, o).start()
            back_core(half, 0).start()

    def gather_1():
        for half in range(2):
            for o in (1, 2, 3):
                back1(half, o).wait_recv()
                back_core(half, o).start()

    def send_grad(a, k):
        return remote(
            grad_send.at[a, k], grad_home.at[a, head], g_s.at[a, k], g_r.at[a, k], at(z_=own_z(k))
        )

    def give_grad(a, k, value):
        grad_send[a, k] = value

        @pl.when(k == 0)
        def _():
            grad_home[a, head] = grad_send[a, 0]

    def query_block(k, carry):
        @pl.when(k == 2)
        def _():
            weight_term()

        @pl.when(k == 3)
        def _():
            sum_core()

        sl = slot(own_z(k), core)
        first, count = block_range(k)
        query, grad = qd[sl, 0], qd[sl, 1]
        lse = lse_col[k][:, :1]
        rd = dot_col[k][:, :1]
        acc = jnp.zeros((TOK, HEAD), F32)
        for t in range(MOST):
            other = nth(first, count, t)
            keys = kv[other, 0]
            p = jnp.exp2(dot(query, keys, NT) * SCALE2 - (lse + pen(t, count)))
            ds = (p * (dot(grad, kv[other, 1], NT) - rd)).astype(BF16)
            acc = acc + dot(ds, keys, NN)
        give_grad(0, k, (acc * FACTOR).astype(BF16))

        @pl.when(k > 0)
        def _():
            send_grad(0, k).start()

        return carry

    lax.fori_loop(0, 4, query_block, 0)

    sum_1()
    for m in range(CROSS):
        spread_cross(1, m)
    all_here(1)
    sum_2()
    for i in range(7):
        send_stats(i).wait_recv()

    def key_block(k, carry):
        @pl.when(k == 1)
        def _():
            sum_z()

        @pl.when(k == 2)
        def _():
            gather_z()

        sl = slot(own_z(k), core)
        first, count = block_range(k)
        keys, values = kv[sl, 0], kv[sl, 1]
        acc_k = jnp.zeros((TOK, HEAD), F32)
        acc_v = jnp.zeros((TOK, HEAD), F32)
        for t in range(MOST):
            other = nth(first, count, t)
            block = other + 6 * yh
            oz = (block // 2) % 8
            left = (2 * head - oz + 8) % 8
            in_left = left < 4
            k_of = jnp.where(in_left, left, 7 - left)
            who = (block // 16) * 4 + jnp.where(in_left, 0, 2) + block % 2
            lse = stats[who, k_of, 0:1, :]
            rd = stats[who, k_of, 8:9, :]
            query, grad = qd[other, 0], qd[other, 1]
            p = jnp.exp2(dot(keys, query, NT) * SCALE2 - (lse + pen(t, count)))
            acc_v = acc_v + dot(p.astype(BF16), grad, NN)
            ds = (p * (dot(values, grad, NT) - rd)).astype(BF16)
            acc_k = acc_k + dot(ds, query, NN)
        give_grad(1, k, (acc_k * FACTOR).astype(BF16))
        give_grad(2, k, acc_v.astype(BF16))

        @pl.when(k >= 1)
        def _():
            for a in (1, 2):
                send_grad(a, k).start()

        return carry

    lax.fori_loop(0, 4, key_block, 0)

    def home_grad(a, k):
        t = targets[k]
        return remote(
            grad_send.at[a, k], grad_home.at[a, t // 2], g_s.at[a, k], g_r.at[a, k], at(z_=t)
        )

    stores = []

    def store(src, dst):
        copy = pltpu.make_async_copy(src, dst, out_s.at[len(stores)])
        copy.start()
        stores.append(copy)

    def finish(a, dst):
        for k in (1, 2, 3):
            home_grad(a, k).wait_recv()
        for h in range(HEADS):
            store(grad_home.at[a, h], dst.at[:, pl.ds(h * HEAD, HEAD)])

    gather_2()
    projected = dot(out_home[0], w_ref[0:HEAD], NN)
    for h in range(1, HEADS):
        projected = projected + dot(out_home[h], w_ref[h * HEAD : (h + 1) * HEAD], NN)
    proj_ref[...] = projected.astype(BF16)
    store(proj_ref, proj_hbm)
    finish(0, gq_hbm)
    gather_1()

    def store_weight(c):
        for half in range(2):
            rows, cols = pl.ds(pl.multiple_of(c * 256, 256), 256), pl.ds(half * 512, 512)
            store(gwf.at[c, half], gw_hbm.at[rows, cols])

    store_weight(core)
    finish(1, gk_hbm)
    finish(2, gv_hbm)
    for half in range(2):
        for o in range(4):
            back_core(half, o).wait_recv()
    store_weight(1 - core)
    for copy in stores:
        copy.wait()

    for k in (1, 2, 3):
        for kind in range(3):
            leg1(kind, k).wait_send()
        send_out(k).wait_send()
        for a in range(3):
            send_grad(a, k).wait_send()
    for g in range(2):
        for k in range(4):
            leg2(g, k).wait_send()
            core1(g, k).wait_send()
            core2(g, k).wait_send()
        for m in range(CROSS):
            leg3(g, m).wait_send()
            cross_core(g, m).wait_send()
    for i in range(7):
        send_stats(i).wait_send()
    ar_core().wait_send()
    for o in (1, 2, 3):
        for half in range(2):
            for make in (step1, step2, back2, back1):
                make(half, o).wait_send()
    for o in range(1, 8):
        ar_z(o).wait_send()
        back_z(o).wait_send()
    for half in range(2):
        for o in range(4):
            back_core(half, o).wait_send()


def hand_on(*refs):
    held, in_sems, out_sems = refs[10:15], refs[15], refs[16]
    copies = []
    for src, dst, mid in zip(refs[:5], refs[5:10], held):
        rows = src.shape[0] // 2
        for part in range(2):
            piece, i = pl.ds(part * rows, rows), len(copies)
            copies.append(
                (
                    pltpu.make_async_copy(src.at[piece], mid.at[piece], in_sems.at[i]),
                    pltpu.make_async_copy(mid.at[piece], dst.at[piece], out_sems.at[i]),
                )
            )
    for come, _ in copies:
        come.start()
    for come, go in copies:
        come.wait()
        go.start()
    for _, go in copies:
        go.wait()


def on_device(query_rows, key_rows, value_rows, recordings, out_weight, cotangent):
    vmem = pltpu.VMEM
    smem = pl.BlockSpec(memory_space=pltpu.SMEM)
    hbm = pl.BlockSpec(memory_space=pl.ANY)
    dma = pltpu.SemaphoreType.DMA
    shapes = [(TOK, D), (TOK, ATT), (TOK, ATT), (TOK, ATT), (ATT, D)]
    shapes = tuple(jax.ShapeDtypeStruct(shape, BF16) for shape in shapes)
    results = pl.pallas_call(
        kernel,
        out_shape=shapes,
        in_specs=[smem, hbm, hbm, hbm, hbm, hbm],
        out_specs=(hbm,) * 5,
        scratch_shapes=[
            vmem((TOK, D), BF16),
            vmem((ATT, D), BF16),
            vmem((TOK, D), BF16),
            pltpu.SMEM((2, 4), jnp.int32),
            vmem((WINDOW, 2, TOK, HEAD), BF16),
            vmem((WINDOW, 2, TOK, HEAD), BF16),
            vmem((HEADS, 2, TOK, HEAD), BF16),
            vmem((HEADS, TOK, HEAD), BF16),
            vmem((HEADS, TOK, HEAD), BF16),
            vmem((8, 4, 16, TOK), F32),
            vmem((4, TOK, HEAD), F32),
            vmem((4, TOK, HEAD), F32),
            vmem((MOST, TOK, TOK), F32),
            vmem((4, TOK, HEAD), BF16),
            vmem((HEADS, TOK, HEAD), BF16),
            vmem((3, 4, TOK, HEAD), BF16),
            vmem((3, HEADS, TOK, HEAD), BF16),
            vmem((2, 2, 4, 4, 16, 512), BF16),
            vmem((2, 4, 4, 16, 512), BF16),
            vmem((2, 4, 4, 16, 512), BF16),
            vmem((2, 4, 16, 512), BF16),
            vmem((2, 3, 4, 16, 512), BF16),
            vmem((2, 3, 16, 512), BF16),
            vmem((8, 16, HEAD), BF16),
            vmem((7, 16, HEAD), BF16),
            vmem((8, 16, HEAD), BF16),
            vmem((2, 2, 256, 512), BF16),
        ]
        + [dma((3, 4))] * 2
        + [dma((2, 4))] * 6
        + [dma((2, CROSS))] * 4
        + [dma((7,))] * 2
        + [dma((4,))] * 2
        + [dma((3, 4))] * 2
        + [dma((5, 2, 4))] * 2
        + [dma((2, 8))] * 2
        + [dma((2, 4))] * 2
        + [dma((14,)), dma((17,))],
        compiler_params=pltpu.CompilerParams(
            collective_id=0, has_side_effects=True, vmem_limit_bytes=56 << 20
        ),
    )(recordings, query_rows[0], key_rows[0], value_rows[0], cotangent[0], out_weight)
    projected, grad_query, grad_key, grad_value, grad_weight = pl.pallas_call(
        hand_on,
        out_shape=shapes,
        in_specs=[hbm] * 5,
        out_specs=(hbm,) * 5,
        scratch_shapes=[vmem(shape.shape, BF16) for shape in shapes] + [dma((10,))] * 2,
    )(*results)
    return (projected[None], grad_query[None], grad_key[None], grad_value[None], grad_weight)


def solution(mesh):
    rows = P("dp", "ctx", None)
    return jax.shard_map(
        on_device,
        mesh=mesh,
        in_specs=(rows, rows, rows, P("dp", None), P(), rows),
        out_specs=(rows, rows, rows, rows, P()),
        check_vma=False,
    )
```
